256 devices in a mesh: vocab: 16 (over y_lo, x, core), dp: 16 (over z, y_hi).
Axes of the slice: x: 4, y: 4 (y_hi: 2, y_lo: 2; y = y_hi * 2 + y_lo), z: 8, core: 2. Of those that a mesh axis runs over, the one named last changes fastest.
Arguments:
- features: bfloat16 [4096, 4096], P('dp'), may hold values from -6 to 6
- token_ids: int32 [4096], P('dp'), may hold values from 0 to 16383
- positions: int32 [4096], replicated, may hold values from 0 to 4095, each once
- target_buffer: bfloat16 [4096, 16384], P(None, ('vocab', 'dp')), may hold values from -96 to 320
- norm_gain: float32 [4096], replicated, may hold values from 0.25 to 1.75
- final_gain: float32 [4096], replicated, may hold values from 0.25 to 1.75
- w_in: bfloat16 [4096, 7168], P(None, 'vocab'), may hold values from -0.09375 to 0.09375
- w_out: bfloat16 [7168, 4096], P('vocab'), may hold values from -0.0625 to 0.0625
- head_weight: bfloat16 [4096, 16384], P('dp', 'vocab'), may hold values from -4 to 4
Outputs:
- grad_head: float32 [4096, 16384], P('dp', 'vocab')
- grad_in: float32 [4096, 7168], P('dp', 'vocab')
- grad_out: float32 [7168, 4096], P('vocab', 'dp')
The draws below stay inside these ranges and needn't reach their ends.
All inputs are finite; a program needn't handle non-finite values.
Results may differ from the reference program's by a relative error of at most 0.04.
Values may be sent and summed in bfloat16 or wider, within the bound.
A program may use at most 128 MiB of HBM per device.

```python
import jax
import jax.numpy as jnp
from jax import lax

D = 4096
FF = 7168
V = 16384
TOK_DEV = 256
TOKENS = 4096
N_VOCAB = 16
N_DP = 16


def draw_target_buffer(key, part):
    key = jax.random.fold_in(key, 7)
    base = 3.0 * jax.random.normal(jax.random.fold_in(key, 1), (TOKENS, V), jnp.float32)
    return jnp.clip(base, -96.0, 320.0).astype(jnp.bfloat16)


def draw_head_weight(key, part):
    key = jax.random.fold_in(key, 13)
    base = jax.random.normal(jax.random.fold_in(key, 1), (D, V), jnp.float32) * D ** (-0.5)
    return jnp.clip(base, -4.0, 4.0).astype(jnp.bfloat16)


def touch_ends(values, rng, low, largest):
    longest = values.shape.index(max(values.shape))
    spots = []
    for shift in (0, 1):
        where = [jax.random.randint(jax.random.fold_in(rng, axis), (), 0, length) for axis, length in enumerate(values.shape)]
        where[longest] = (where[longest] + shift) % values.shape[longest]
        spots.append(tuple(where))
    return values.at[spots[0]].set(low).at[spots[1]].set(largest)


def level_of(stream_key, shape, split, low, largest):
    factor_of = 1.0
    for position, parts in split:
        draws = jax.random.uniform(jax.random.fold_in(jax.random.fold_in(stream_key, 6), position), (parts,), jnp.float32, low / len(split), largest / len(split))
        factor_of = factor_of * jnp.repeat(jnp.exp(draws), shape[position] // parts).reshape((-1,) + (1,) * (len(shape) - 1 - position))
    return factor_of


def noise(key, dims, scale, most, cuts=(), kind=jnp.bfloat16):
    entries = scale * jax.random.normal(key, dims, jnp.float32)
    if cuts:
        entries = entries * level_of(key, dims, cuts, -0.22, 0.18)
    return jnp.clip(entries, -most, most).astype(kind)


def setup_inputs(seed: int = 0) -> dict:
    arg_keys = jax.random.split(jax.random.key(seed), 10)
    features = noise(arg_keys[0], (TOKENS, D), 1.0, 6.0, ((0, 16),))
    token_ids = touch_ends(jax.random.randint(arg_keys[1], (TOKENS,), 0, V), jax.random.fold_in(arg_keys[1], 1), 0, V - 1).astype(jnp.int32)
    positions = jax.random.permutation(arg_keys[2], TOKENS).astype(jnp.int32)
    target_buffer = draw_target_buffer(jax.random.fold_in(arg_keys[9], 71), 0)
    norm_gain = jnp.clip(1.0 + 0.15 * jax.random.normal(arg_keys[4], (D,), jnp.float32), 0.25, 1.75)
    final_gain = jnp.clip(1.0 + 0.15 * jax.random.normal(arg_keys[5], (D,), jnp.float32), 0.25, 1.75)
    w_in = noise(arg_keys[6], (D, FF), D ** -0.5, 0.09375, ((1, 16),))
    w_out = noise(arg_keys[7], (FF, D), FF ** -0.5, 0.0625, ((0, 16),))
    head_weight = draw_head_weight(jax.random.fold_in(arg_keys[9], 71), 0)
    return dict(features=features, token_ids=token_ids, positions=positions, target_buffer=target_buffer, norm_gain=norm_gain, final_gain=final_gain, w_in=w_in, w_out=w_out, head_weight=head_weight)


EPS = 1e-05
HARD = 0.5

def rounded(value):
    return lax.optimization_barrier(value.astype(jnp.bfloat16)).astype(jnp.float32)

def reference(features, token_ids, positions, target_buffer, norm_gain, final_gain, w_in, w_out, head_weight):
    target = target_buffer[positions]
    xfloat = features.astype(jnp.float32)
    rinput = lax.rsqrt(lax.optimization_barrier(jnp.mean(xfloat * xfloat, -1, keepdims=True)) + EPS)
    normed = (xfloat * rinput * norm_gain).astype(jnp.bfloat16)
    pre = jnp.dot(normed, w_in, preferred_element_type=jnp.float32)
    act = jax.nn.silu(pre).astype(jnp.bfloat16)
    width = FF // N_VOCAB
    hidden = jnp.zeros(xfloat.shape, jnp.float32)
    for block in range(N_VOCAB):
        hidden = hidden + rounded(jnp.dot(act[:, block * width:(block + 1) * width], w_out[block * width:(block + 1) * width], preferred_element_type=jnp.float32))
    resid = xfloat + hidden
    rscale = lax.rsqrt(lax.optimization_barrier(jnp.mean(resid * resid, -1, keepdims=True)) + EPS)
    final = (resid * rscale * final_gain).astype(jnp.bfloat16)
    logits = jnp.dot(final, head_weight, preferred_element_type=jnp.float32)
    tfloat = target.astype(jnp.float32)
    qexp = jnp.exp(logits - lax.optimization_barrier(jnp.max(logits, -1, keepdims=True)))
    qprob = qexp / lax.optimization_barrier(jnp.sum(qexp, -1, keepdims=True))
    pexp = jnp.exp(tfloat - lax.optimization_barrier(jnp.max(tfloat, -1, keepdims=True)))
    pprob = pexp / lax.optimization_barrier(jnp.sum(pexp, -1, keepdims=True))
    onehot = (jnp.arange(V, dtype=jnp.int32)[None, :] == token_ids[:, None]).astype(jnp.float32)
    dlogits = (qprob - pprob + HARD * (qprob - onehot)).astype(jnp.bfloat16)
    vwidth = V // N_VOCAB
    dfinal = jnp.zeros(xfloat.shape, jnp.float32)
    for block in range(N_VOCAB):
        cols = slice(block * vwidth, (block + 1) * vwidth)
        dfinal = dfinal + rounded(lax.dot_general(dlogits[:, cols], head_weight[:, cols], (((1,), (1,)), ((), ())), preferred_element_type=jnp.float32))
    inner = lax.optimization_barrier(jnp.sum(dfinal * final_gain * resid, -1, keepdims=True))
    dresid = (rscale * final_gain * dfinal - resid * rscale ** 3 / D * inner).astype(jnp.bfloat16)
    dact = lax.dot_general(dresid, w_out, (((1,), (1,)), ((), ())), preferred_element_type=jnp.float32)
    sig = jax.nn.sigmoid(pre)
    dpre = (dact * sig * (1.0 + pre * (1.0 - sig))).astype(jnp.bfloat16)
    grad_head = jnp.zeros((D, V), jnp.float32)
    grad_in = jnp.zeros((D, FF), jnp.float32)
    grad_out = jnp.zeros((FF, D), jnp.float32)
    contract = (((0,), (0,)), ((), ()))
    for group in range(N_DP):
        rows = slice(group * TOK_DEV, (group + 1) * TOK_DEV)
        grad_head = grad_head + rounded(lax.dot_general(final[rows], dlogits[rows], contract, preferred_element_type=jnp.float32))
        grad_in = grad_in + rounded(lax.dot_general(normed[rows], dpre[rows], contract, preferred_element_type=jnp.float32))
        grad_out = grad_out + rounded(lax.dot_general(act[rows], dresid[rows], contract, preferred_element_type=jnp.float32))
    return (grad_head, grad_in, grad_out)
```

```python
import jax
import jax.numpy as jnp
from jax import lax
from jax.sharding import Mesh, PartitionSpec as P

EPS = 1e-05
HARD = 0.5
PLANE = ("yhi", "ylo", "x", "core")


def body(
    features, token_ids, positions, target_buffer, norm_gain, final_gain, w_in, w_out, head_weight
):
    yhi = lax.axis_index("yhi")
    vocab = lax.axis_index(("ylo", "x", "core"))
    plane = lax.axis_index(PLANE)
    f32 = jnp.float32
    bf16 = jnp.bfloat16
    backward = (((1,), (1,)), ((), ()))
    contract = (((0,), (0,)), ((), ()))

    rows, cols = head_weight.shape
    hw = head_weight.reshape(rows, 8, 2, cols // 16)
    hw = lax.all_to_all(hw, "yhi", split_axis=2, concat_axis=0, tiled=True)
    hw = hw.reshape(rows * 2, cols // 2)
    full_head = lax.all_gather(hw, "z", axis=0, tiled=True)

    tw = target_buffer.shape[1]
    ordered = target_buffer[positions].reshape(8, -1, tw)
    target = lax.all_to_all(ordered, "z", split_axis=0, concat_axis=2, tiled=True)[0]

    feats = lax.all_gather(features, "yhi", axis=0, tiled=True)
    toks = lax.all_gather(token_ids, "yhi", axis=0, tiled=True)
    n_tok, width = feats.shape
    xfloat = feats.astype(f32)
    rinput = lax.rsqrt(jnp.mean(xfloat * xfloat, -1, keepdims=True) + EPS)
    normed = (xfloat * rinput * norm_gain).astype(bf16)
    fw = w_in.shape[1] // 2
    win = lax.dynamic_slice_in_dim(w_in, yhi * fw, fw, 1)
    wout = lax.dynamic_slice_in_dim(w_out, yhi * fw, fw, 0)
    pre = jnp.dot(normed, win, preferred_element_type=f32)
    act = jax.nn.silu(pre).astype(bf16)
    part = jnp.dot(act, wout, preferred_element_type=f32).astype(bf16)
    hidden = lax.psum_scatter(part, PLANE, scatter_dimension=0, tiled=True).astype(f32)
    own = hidden.shape[0]
    xown = lax.dynamic_slice_in_dim(feats, plane * own, own, 0).astype(f32)
    resid = xown + hidden
    rscale = lax.rsqrt(jnp.mean(resid * resid, -1, keepdims=True) + EPS)
    final = (resid * rscale * final_gain).astype(bf16)
    final = lax.all_gather(final, PLANE, axis=0, tiled=True)

    logits = jnp.dot(final, full_head, preferred_element_type=f32)
    tfloat = target.astype(f32)
    top_q = jnp.max(logits, -1)
    top_p = jnp.max(tfloat, -1)
    qexp = jnp.exp(logits - top_q[:, None])
    pexp = jnp.exp(tfloat - top_p[:, None])
    stats = jnp.stack([top_q, jnp.sum(qexp, -1), top_p, jnp.sum(pexp, -1)])
    every = lax.all_gather(stats, PLANE, axis=0)
    all_q = jnp.max(every[:, 0], 0)
    all_p = jnp.max(every[:, 2], 0)
    sum_q = jnp.sum(every[:, 1] * jnp.exp(every[:, 0] - all_q), 0)
    sum_p = jnp.sum(every[:, 3] * jnp.exp(every[:, 2] - all_p), 0)
    qprob = qexp * (jnp.exp(top_q - all_q) / sum_q)[:, None]
    pprob = pexp * (jnp.exp(top_p - all_p) / sum_p)[:, None]
    lane = jnp.arange(cols // 2, dtype=jnp.int32)
    columns_here = vocab * cols + (lane // tw) * (2 * tw) + yhi * tw + lane % tw
    onehot = (columns_here[None, :] == toks[:, None]).astype(f32)
    dlogits = (qprob - pprob + HARD * (qprob - onehot)).astype(bf16)

    part = lax.dot_general(dlogits, full_head, backward, preferred_element_type=f32).astype(bf16)
    dfinal = lax.psum_scatter(part, PLANE, scatter_dimension=0, tiled=True).astype(f32)
    inner = jnp.sum(dfinal * final_gain * resid, -1, keepdims=True)
    dresid = (rscale * final_gain * dfinal - resid * rscale**3 / width * inner).astype(bf16)
    dresid = lax.all_gather(dresid, PLANE, axis=0, tiled=True)

    gh = lax.dot_general(final, dlogits, contract, preferred_element_type=f32).astype(bf16)
    gh = lax.psum_scatter(gh, "z", scatter_dimension=0, tiled=True)
    gh = lax.all_to_all(
        gh.reshape(rows * 2, 8, 1, tw), "yhi", split_axis=0, concat_axis=2, tiled=True
    ).reshape(rows, cols).astype(f32)

    dact = lax.dot_general(dresid, wout, backward, preferred_element_type=f32)
    sig = jax.nn.sigmoid(pre)
    dpre = (dact * sig * (1.0 + pre * (1.0 - sig))).astype(bf16)
    gf = jnp.concatenate(
        [
            lax.dot_general(normed, dpre, contract, preferred_element_type=f32),
            lax.dot_general(dresid, act, contract, preferred_element_type=f32),
        ],
        1,
    ).astype(bf16)
    gf = lax.psum_scatter(gf, "z", scatter_dimension=0, tiled=True)
    gf = lax.all_to_all(
        gf.reshape(rows * 2, 2, fw), "yhi", split_axis=0, concat_axis=2, tiled=True
    ).astype(f32)
    return (gh, gf[:, 0], gf[:, 1].T)


def solution(mesh):
    names = ("ylo", "x", "core", "z", "yhi")
    fine = Mesh(mesh.devices.reshape(2, 4, 2, 8, 2), names)
    v = ("ylo", "x", "core")
    d = ("z", "yhi")
    return jax.shard_map(
        body,
        mesh=fine,
        in_specs=(
            P(d, None),
            P(d),
            P(),
            P(None, v + d),
            P(),
            P(),
            P(None, v),
            P(v, None),
            P(d, v),
        ),
        out_specs=(P(d, v), P(d, v), P(v, d)),
        check_vma=False,
    )
```

```python
import functools
import jax
import jax.numpy as jnp
from jax import lax
from jax.experimental import pallas as pl
from jax.experimental.pallas import tpu as pltpu
from jax.sharding import Mesh, PartitionSpec as P

EPS = 1e-05
HARD = 0.5
MESH = pl.DeviceIdType.MESH
LEAD = ("YB", "core", "XA", "YA", "XB")
BLK = 16


def place():
    x, ylo, yhi, core = (lax.axis_index(n) for n in ("x", "ylo", "yhi", "core"))
    y = 2 * yhi + ylo
    odd = lax.rem(x, 2)
    bits = {
        "core": core,
        "XA": lax.rem(lax.div(x + 1, 2), 2),
        "XB": lax.div(x, 2),
        "YA": lax.rem(lax.div(y + 1, 2), 2),
        "YB": yhi,
    }
    to = {
        "core": {"core": 1 - core},
        "XA": {"x": x + 1 - 2 * odd},
        "XB": {"x": lax.rem(x + 3 + 2 * odd, 4)},
        "YA": {"ylo": 1 - ylo},
        "YB": {"ylo": 1 - ylo, "yhi": 1 - yhi},
    }
    return bits, to


def at(names, fixed, cols=None):
    where = tuple(fixed.get(n, slice(None)) for n in names)
    return where + (slice(None), slice(None) if cols is None else pl.ds(*cols))


def corners(names):
    out = [{}]
    for n in names:
        out = [dict(o, **{n: v}) for o in out for v in (0, 1)]
    return out


class Sender:
    def __init__(self, send_sem, recv_sem, to):
        self.send_sem, self.recv_sem, self.to = send_sem, recv_sem, to
        self.n = 0
        self.all = []

    def go(self, src, dst, dim):
        c = pltpu.make_async_remote_copy(
            src_ref=src,
            dst_ref=dst,
            send_sem=self.send_sem.at[self.n],
            recv_sem=self.recv_sem.at[self.n],
            device_id=self.to[dim],
            device_id_type=MESH,
        )
        c.start()
        self.n += 1
        self.all.append(c)
        return c

    def drain(self):
        for c in self.all:
            c.wait_send()


def colours(n, width):
    tiles = width // 128
    edges = [128 * (tiles * k // n) for k in range(n + 1)]
    return [(edges[k], edges[k + 1] - edges[k]) for k in range(n)]


def meet(to):
    barrier = pltpu.get_barrier_semaphore()
    for d in LEAD:
        pl.semaphore_signal(barrier, inc=1, device_id=to[d], device_id_type=MESH)
    pl.semaphore_wait(barrier, len(LEAD))


def reduce_cube(send, bits, names, dims, width, part, total, landed):
    rest = tuple(n for n in names if n != "core")
    n = len(dims)
    cuts = colours(n, width)
    first, second = [], []
    for keep, held in ((1, first), (0, second)):
        for k in range(n):
            d = dims[k]
            bit = 1 - bits[d] if keep else bits[d]
            src = part.at[at(names, {"core": 1 - bits["core"], d: bit}, cuts[k])]
            dst = total.at[at(rest, {d: bit}, cuts[k])]
            held.append(send.go(src, dst, "core"))

    def merge(k, bit):
        d = dims[k]
        for f in corners([m for m in rest if m != d]):
            f = dict(f, **{d: bit})
            w = at(rest, f, cuts[k])
            total[w] = total[w] + part[at(names, dict(f, core=bits["core"]), cuts[k])]

    def start(k, j):
        d = dims[(k + j) % n]
        fixed = {dims[(k + i) % n]: bits[dims[(k + i) % n]] for i in range(j)}
        fixed[d] = 1 - bits[d]
        return send.go(total.at[at(rest, fixed, cuts[k])], landed[k * n + j], d)

    flying = []
    for k in range(n):
        first[k].wait_recv()
        merge(k, 1 - bits[dims[k]])
        flying.append(start(k, 0))
    for k in range(n):
        second[k].wait_recv()
        merge(k, bits[dims[k]])
    for j in range(n):
        for k in range(n):
            flying[k].wait_recv()
            done = [dims[(k + i) % n] for i in range(j + 1)]
            fixed = {m: bits[m] for m in done}
            left = [m for m in rest if m not in done]
            for f in corners(left):
                w = at(rest, dict(f, **fixed), cuts[k])
                total[w] = total[w] + landed[k * n + j][tuple(f[m] for m in left)]
            if j + 1 < n:
                flying[k] = start(k, j + 1)


def gather_cube(send, bits, dims, width, full):
    n = len(dims)
    cuts = colours(n, width)
    arriving = [send.go(full.at[at(LEAD, bits)], full.at[at(LEAD, bits)], "core")]
    for j in range(n):
        flying = []
        for k in range(n):
            d = dims[(k + j) % n]
            done = [dims[(k + i) % n] for i in range(j)]
            piece = full.at[at(LEAD, {m: bits[m] for m in LEAD if m not in done}, cuts[k])]
            flying.append(send.go(piece, piece, d))
        for k in range(n):
            flying[k].wait_recv()
            d = dims[(k + j) % n]
            done = [dims[(k + i) % n] for i in range(j)]
            fixed = {m: bits[m] for m in LEAD if m not in done}
            fixed[d] = 1 - bits[d]
            piece = full.at[at(LEAD, fixed, cuts[k])]
            arriving.append(send.go(piece, piece, "core"))
    for c in arriving:
        c.wait_recv()


ICI3 = ("XA", "YA", "XB")
ICI4 = ("XA", "YA", "XB", "YB")


def landing(dims, width):
    n = len(dims)
    cuts = colours(n, width)
    return [
        pltpu.VMEM((2,) * (n - 1 - j) + (BLK, cuts[k][1]), jnp.bfloat16)
        for k in range(n)
        for j in range(n)
    ]


def forward_kernel(
    width, run, part, feats, gain, final_own, final_pair, resid_out, scale_out,
    total, full, xown, send_sem, recv_sem, local_sem, *landed,
):
    bits, to = place()
    names = LEAD[1:]
    mine = at(names, bits)
    fetch = pltpu.make_async_copy(feats.at[mine], xown, local_sem.at[0])
    fetch.start()
    meet(to)
    send = Sender(send_sem, recv_sem, to)
    reduce_cube(send, bits, names, ICI3, width, part, total, landed)
    fetch.wait()
    hidden = total[at(ICI3, bits)].astype(jnp.float32)
    resid = xown[...].astype(jnp.float32) + hidden
    rscale = lax.rsqrt(jnp.mean(resid * resid, -1, keepdims=True) + EPS)
    resid_out[...] = resid
    scale_out[...] = jnp.broadcast_to(rscale, scale_out.shape)
    full[at(LEAD, bits)] = (resid * rscale * gain[...]).astype(jnp.bfloat16)
    gather_cube(send, bits, ICI4, width, full)
    out = []
    for b in range(width // (2 * run)):
        for s, ref in ((bits["YB"], final_own), (1 - bits["YB"], final_pair)):
            c = pltpu.make_async_copy(
                full.at[at(LEAD, {}, (pl.multiple_of((2 * b + s) * run, run), run))],
                ref.at[at(LEAD, {}, (b * run, run))],
                local_sem.at[1 + len(out)],
            )
            c.start()
            out.append(c)
    for c in out:
        c.wait()
    send.drain()


def backward_kernel(
    width, run, part_own, part_pair, resid, scale, gain, grad_own, grad_half,
    part, total, full, send_sem, recv_sem, local_sem, *landed,
):
    bits, to = place()
    runs = width // (2 * run)
    fetch = []
    for b in range(runs):
        for s, ref in ((bits["YB"], part_own), (1 - bits["YB"], part_pair)):
            c = pltpu.make_async_copy(
                ref.at[at(LEAD, {}, (b * run, run))],
                part.at[at(LEAD, {}, (pl.multiple_of((2 * b + s) * run, run), run))],
                local_sem.at[len(fetch)],
            )
            c.start()
            fetch.append(c)
    meet(to)
    for c in fetch:
        c.wait()
    send = Sender(send_sem, recv_sem, to)
    reduce_cube(send, bits, LEAD, ICI4, width, part, total, landed)
    rest = tuple(n for n in LEAD if n != "core")
    dfinal = total[at(rest, bits)].astype(jnp.float32)
    r = resid[...]
    rscale = scale[...][:, :1]
    scaled = dfinal * gain[...]
    inner = jnp.sum(scaled * r, -1, keepdims=True)
    full[at(LEAD, bits)] = (rscale * scaled - r * (rscale * rscale * rscale / width * inner)).astype(
        jnp.bfloat16
    )
    gather_cube(send, bits, ICI4, width, full)
    out = [
        pltpu.make_async_copy(full.at[at(LEAD, {"YB": bits["YB"]})], grad_own, local_sem.at[2 * runs])
    ]
    for b in range(runs):
        for s, slot in ((bits["YB"], 0), (1 - bits["YB"], 1)):
            col = pl.multiple_of((2 * b + bits["YB"]) * run, run)
            out.append(
                pltpu.make_async_copy(
                    full.at[at(LEAD, {"YB": s}, (col, run))],
                    grad_half.at[at(LEAD, {"YB": slot}, (b * run, run))],
                    local_sem.at[len(out) - 1],
                )
            )
    for c in out:
        c.start()
    for c in out:
        c.wait()
    send.drain()


def stats_kernel(stats, out, near, far, held, send_sem, recv_sem):
    x, ylo, yhi, core = (lax.axis_index(n) for n in ("x", "ylo", "yhi", "core"))
    row = [
        {"x": lax.rem(x + i, 4), "core": lax.rem(core + c, 2)}
        for i in range(4) for c in range(2) if i or c
    ]
    column = [
        {"ylo": lax.rem(ylo + a, 2), "yhi": lax.rem(yhi + b, 2)}
        for a in range(2) for b in range(2) if a or b
    ]
    barrier = pltpu.get_barrier_semaphore()
    for d in row + column:
        pl.semaphore_signal(barrier, inc=1, device_id=d, device_id_type=MESH)
    pl.semaphore_wait(barrier, len(row) + len(column))

    def exchange(src, slots, peers, base):
        flying = []
        for i, d in enumerate(peers):
            c = pltpu.make_async_remote_copy(
                src_ref=src,
                dst_ref=slots.at[i],
                send_sem=send_sem.at[base + i],
                recv_sem=recv_sem.at[base + i],
                device_id=d,
                device_id_type=MESH,
            )
            c.start()
            flying.append(c)
        for c in flying:
            c.wait_recv()
        parts = [src[...]] + [slots[i] for i in range(len(peers))]
        tops = [p[0:2] for p in parts]
        top = functools.reduce(jnp.maximum, tops)
        total = functools.reduce(
            jnp.add, [p[2:4] * jnp.exp(t - top) for p, t in zip(parts, tops)]
        )
        return flying, top, total

    one, top, total = exchange(stats, near, row, 0)
    held[0:2] = top
    held[2:4] = total
    held[4:8] = jnp.zeros((4, held.shape[1]), jnp.float32)
    two, top, total = exchange(held, far, column, len(row))
    out[0:2] = top
    out[2:4] = total
    out[4:8] = jnp.zeros((4, out.shape[1]), jnp.float32)
    for c in one + two:
        c.wait_send()


VM = pl.BlockSpec(memory_space=pltpu.VMEM)
ANY = pl.BlockSpec(memory_space=pl.ANY)
CUBE = (2,) * 5


def params(cid):
    return pltpu.CompilerParams(
        collective_id=cid, has_side_effects=True, vmem_limit_bytes=40 * 1024 * 1024
    )


def call_forward(part, feats, gain, run):
    width = part.shape[1]
    sd = jax.ShapeDtypeStruct
    bf16, f32 = jnp.bfloat16, jnp.float32
    n_sem = 6 + 9 + 1 + 32
    own, pair, resid, scale = pl.pallas_call(
        functools.partial(forward_kernel, width, run),
        out_shape=(
            sd(CUBE + (BLK, width // 2), bf16),
            sd(CUBE + (BLK, width // 2), bf16),
            sd((BLK, width), f32),
            sd((BLK, 128), f32),
        ),
        in_specs=[VM, ANY, VM],
        out_specs=(ANY, ANY, VM, VM),
        scratch_shapes=[
            pltpu.VMEM((2,) * 3 + (BLK, width), bf16),
            pltpu.VMEM(CUBE + (BLK, width), bf16),
            pltpu.VMEM((BLK, width), bf16),
            pltpu.SemaphoreType.DMA((n_sem,)),
            pltpu.SemaphoreType.DMA((n_sem,)),
            pltpu.SemaphoreType.DMA((1 + width // run,)),
        ]
        + landing(ICI3, width),
        compiler_params=params(1),
        cost_estimate=pl.CostEstimate(flops=10**6, bytes_accessed=10**8, transcendentals=0),
        name="forward_plane",
    )(part.reshape(CUBE[1:] + (BLK, width)), feats.reshape(CUBE[1:] + (BLK, width)), gain[None])
    return own.reshape(-1, width // 2), pair.reshape(-1, width // 2), resid, scale


def call_backward(part_own, part_pair, resid, scale, gain, run):
    width = resid.shape[1]
    sd = jax.ShapeDtypeStruct
    bf16 = jnp.bfloat16
    n_sem = 8 + 16 + 1 + 32
    half = CUBE + (BLK, width // 2)
    own, halves = pl.pallas_call(
        functools.partial(backward_kernel, width, run),
        out_shape=(sd(CUBE[1:] + (BLK, width), bf16), sd(half, bf16)),
        in_specs=[ANY, ANY, VM, VM, VM],
        out_specs=(ANY, ANY),
        scratch_shapes=[
            pltpu.VMEM(CUBE + (BLK, width), bf16),
            pltpu.VMEM((2,) * 4 + (BLK, width), bf16),
            pltpu.VMEM(CUBE + (BLK, width), bf16),
            pltpu.SemaphoreType.DMA((n_sem,)),
            pltpu.SemaphoreType.DMA((n_sem,)),
            pltpu.SemaphoreType.DMA((1 + width // run,)),
        ]
        + landing(ICI4, width),
        compiler_params=params(3),
        cost_estimate=pl.CostEstimate(flops=10**6, bytes_accessed=10**8, transcendentals=0),
        name="backward_plane",
    )(part_own.reshape(half), part_pair.reshape(half), resid, scale, gain[None])
    return own.reshape(-1, width), halves.reshape(-1, width // 2)


def call_stats(stats):
    f32 = jnp.float32
    n = stats.shape[1]
    return pl.pallas_call(
        stats_kernel,
        out_shape=jax.ShapeDtypeStruct((8, n), f32),
        in_specs=[VM],
        out_specs=VM,
        scratch_shapes=[
            pltpu.VMEM((7, 8, n), f32),
            pltpu.VMEM((3, 8, n), f32),
            pltpu.VMEM((8, n), f32),
            pltpu.SemaphoreType.DMA((10,)),
            pltpu.SemaphoreType.DMA((10,)),
        ],
        compiler_params=params(2),
        name="softmax_stats",
    )(stats)


def body(
    features, token_ids, positions, target_buffer, norm_gain, final_gain, w_in, w_out, head_weight
):
    yhi = lax.axis_index("yhi")
    vocab = lax.axis_index(("ylo", "x", "core"))
    f32 = jnp.float32
    bf16 = jnp.bfloat16
    backward = (((1,), (1,)), ((), ()))
    contract = (((0,), (0,)), ((), ()))
    swap = functools.partial(lax.ppermute, axis_name="yhi", perm=[(0, 1), (1, 0)])
    gather = functools.partial(lax.all_gather, axis_name="z", axis=0, tiled=True)
    scatter = functools.partial(lax.psum_scatter, axis_name="z", scatter_dimension=0, tiled=True)

    def pick(array, axis, index):
        return lax.dynamic_index_in_dim(array, index, axis, keepdims=False)

    rows, cols = head_weight.shape
    hw = head_weight.reshape(rows, 8, 2, cols // 16)
    head_pair = swap(pick(hw, 2, 1 - yhi).reshape(rows, cols // 2))
    head_own = gather(pick(hw, 2, yhi).reshape(rows, cols // 2))
    head_pair = gather(head_pair)

    tok, width = features.shape
    xfloat = features.astype(f32)
    rinput = lax.rsqrt(jnp.mean(xfloat * xfloat, -1, keepdims=True) + EPS)
    normed = (xfloat * rinput * norm_gain).astype(bf16)
    pre = jnp.dot(normed, w_in, preferred_element_type=f32)
    act = jax.nn.silu(pre).astype(bf16)
    part = jnp.dot(act, w_out, preferred_element_type=f32).astype(bf16)
    final_own, final_pair, resid, scale = call_forward(part, features, final_gain, rows)

    split = normed.reshape(tok, 8, 2, rows)
    normed_own = pick(split, 2, yhi).reshape(tok, width // 2)
    normed_pair = swap(pick(split, 2, 1 - yhi).reshape(tok, width // 2))
    normed2 = jnp.concatenate([normed_own, normed_pair], 0)
    act2 = jnp.concatenate([act, swap(act)], 0)

    tw = target_buffer.shape[1]
    ordered = target_buffer[positions].reshape(8, -1, tw)
    target = lax.all_to_all(ordered, "z", split_axis=0, concat_axis=2, tiled=True)[0]
    toks = lax.all_gather(token_ids, "yhi", axis=0, tiled=True)

    logits = jnp.dot(final_own, head_own, preferred_element_type=f32) + jnp.dot(
        final_pair, head_pair, preferred_element_type=f32
    )
    tfloat = target.astype(f32)
    top_q = jnp.max(logits, -1)
    top_p = jnp.max(tfloat, -1)
    qexp = jnp.exp(logits - top_q[:, None])
    pexp = jnp.exp(tfloat - top_p[:, None])
    zero = jnp.zeros_like(top_q)
    stats = jnp.stack([top_q, top_p, jnp.sum(qexp, -1), jnp.sum(pexp, -1), zero, zero, zero, zero])
    every = call_stats(stats)
    qprob = qexp * (jnp.exp(top_q - every[0]) / every[2])[:, None]
    pprob = pexp * (jnp.exp(top_p - every[1]) / every[3])[:, None]
    lane = jnp.arange(cols // 2, dtype=jnp.int32)
    columns_here = vocab * cols + (lane // tw) * (2 * tw) + yhi * tw + lane % tw
    onehot = (columns_here[None, :] == toks[:, None]).astype(f32)
    dlogits = (qprob - pprob + HARD * (qprob - onehot)).astype(bf16)

    gh_pair = lax.dot_general(final_pair, dlogits, contract, preferred_element_type=f32).astype(bf16)
    gh_pair = scatter(gh_pair)
    gh_own = lax.dot_general(final_own, dlogits, contract, preferred_element_type=f32).astype(bf16)
    gh_own = scatter(gh_own)
    gh_other = swap(gh_pair)
    both = jnp.stack([gh_own, gh_other]).reshape(2, rows, 8, tw)
    both = jnp.where(yhi == 0, both, both[::-1])
    grad_head = both.transpose(1, 2, 0, 3).reshape(rows, cols).astype(f32)

    part_own = lax.dot_general(dlogits, head_own, backward, preferred_element_type=f32).astype(bf16)
    part_pair = lax.dot_general(dlogits, head_pair, backward, preferred_element_type=f32).astype(bf16)
    dresid, dresid2 = call_backward(part_own, part_pair, resid, scale, final_gain, rows)

    go = lax.dot_general(dresid2, act2, contract, preferred_element_type=f32).astype(bf16)
    go = scatter(go).astype(f32)
    dact = lax.dot_general(dresid, w_out, backward, preferred_element_type=f32)
    sig = jax.nn.sigmoid(pre)
    dpre = (dact * sig * (1.0 + pre * (1.0 - sig))).astype(bf16)
    dpre2 = jnp.concatenate([dpre, swap(dpre)], 0)
    gi = lax.dot_general(normed2, dpre2, contract, preferred_element_type=f32).astype(bf16)
    gi = scatter(gi).astype(f32)
    return (grad_head, gi, go.T)


def solution(mesh):
    names = ("ylo", "x", "core", "z", "yhi")
    fine = Mesh(mesh.devices.reshape(2, 4, 2, 8, 2), names)
    v = ("ylo", "x", "core")
    d = ("z", "yhi")
    return jax.shard_map(
        body,
        mesh=fine,
        in_specs=(
            P(d, None),
            P(d),
            P(),
            P(None, v + d),
            P(),
            P(),
            P(None, v),
            P(v, None),
            P(d, v),
        ),
        out_specs=(P(d, v), P(d, v), P(v, d)),
        check_vma=False,
    )
```

```python
import functools
import jax
import jax.numpy as jnp
from jax import lax
from jax.experimental import pallas as pl
from jax.experimental.pallas import tpu as pltpu
from jax.sharding import Mesh, PartitionSpec as P

EPS = 1e-05
HARD = 0.5
MESH = pl.DeviceIdType.MESH
LEAD = ("YB", "core", "XA", "YA", "XB")
BLK = 16


def place():
    x, ylo, yhi, core = (lax.axis_index(n) for n in ("x", "ylo", "yhi", "core"))
    y = 2 * yhi + ylo
    odd = lax.rem(x, 2)
    bits = {
        "core": core,
        "XA": lax.rem(lax.div(x + 1, 2), 2),
        "XB": lax.div(x, 2),
        "YA": lax.rem(lax.div(y + 1, 2), 2),
        "YB": yhi,
    }
    to = {
        "core": {"core": 1 - core},
        "XA": {"x": x + 1 - 2 * odd},
        "XB": {"x": lax.rem(x + 3 + 2 * odd, 4)},
        "YA": {"ylo": 1 - ylo},
        "YB": {"ylo": 1 - ylo, "yhi": 1 - yhi},
    }
    return bits, to


def at(names, fixed, cols=None):
    where = tuple(fixed.get(n, slice(None)) for n in names)
    return where + (slice(None), slice(None) if cols is None else pl.ds(*cols))


def corners(names):
    out = [{}]
    for n in names:
        out = [dict(o, **{n: v}) for o in out for v in (0, 1)]
    return out


class Sender:
    def __init__(self, send_sem, recv_sem, to):
        self.send_sem, self.recv_sem, self.to = send_sem, recv_sem, to
        self.n = 0
        self.all = []

    def go(self, src, dst, dim):
        c = pltpu.make_async_remote_copy(
            src_ref=src,
            dst_ref=dst,
            send_sem=self.send_sem.at[self.n],
            recv_sem=self.recv_sem.at[self.n],
            device_id=self.to[dim],
            device_id_type=MESH,
        )
        c.start()
        self.n += 1
        self.all.append(c)
        return c

    def drain(self):
        for c in self.all:
            c.wait_send()


def colours(n, width):
    tiles = width // 128
    edges = [128 * (tiles * k // n) for k in range(n + 1)]
    return [(edges[k], edges[k + 1] - edges[k]) for k in range(n)]


def meet(to):
    barrier = pltpu.get_barrier_semaphore()
    for d in LEAD:
        pl.semaphore_signal(barrier, inc=1, device_id=to[d], device_id_type=MESH)
    pl.semaphore_wait(barrier, len(LEAD))


def reduce_cube(send, bits, names, dims, width, part, total, landed):
    rest = tuple(n for n in names if n != "core")
    n = len(dims)
    cuts = colours(n, width)
    first, second = [], []
    for keep, held in ((1, first), (0, second)):
        for k in range(n):
            d = dims[k]
            bit = 1 - bits[d] if keep else bits[d]
            src = part.at[at(names, {"core": 1 - bits["core"], d: bit}, cuts[k])]
            dst = total.at[at(rest, {d: bit}, cuts[k])]
            held.append(send.go(src, dst, "core"))

    def merge(k, bit):
        d = dims[k]
        for f in corners([m for m in rest if m != d]):
            f = dict(f, **{d: bit})
            w = at(rest, f, cuts[k])
            total[w] = total[w] + part[at(names, dict(f, core=bits["core"]), cuts[k])]

    def start(k, j):
        d = dims[(k + j) % n]
        fixed = {dims[(k + i) % n]: bits[dims[(k + i) % n]] for i in range(j)}
        fixed[d] = 1 - bits[d]
        return send.go(total.at[at(rest, fixed, cuts[k])], landed[k * n + j], d)

    flying = []
    for k in range(n):
        first[k].wait_recv()
        merge(k, 1 - bits[dims[k]])
        flying.append(start(k, 0))
    for k in range(n):
        second[k].wait_recv()
        merge(k, bits[dims[k]])
    for j in range(n):
        for k in range(n):
            flying[k].wait_recv()
            done = [dims[(k + i) % n] for i in range(j + 1)]
            fixed = {m: bits[m] for m in done}
            left = [m for m in rest if m not in done]
            for f in corners(left):
                w = at(rest, dict(f, **fixed), cuts[k])
                total[w] = total[w] + landed[k * n + j][tuple(f[m] for m in left)]
            if j + 1 < n:
                flying[k] = start(k, j + 1)


def gather_cube(send, bits, dims, width, full):
    n = len(dims)
    cuts = colours(n, width)
    arriving = [send.go(full.at[at(LEAD, bits)], full.at[at(LEAD, bits)], "core")]
    for j in range(n):
        flying = []
        for k in range(n):
            d = dims[(k + j) % n]
            done = [dims[(k + i) % n] for i in range(j)]
            piece = full.at[at(LEAD, {m: bits[m] for m in LEAD if m not in done}, cuts[k])]
            flying.append(send.go(piece, piece, d))
        for k in range(n):
            flying[k].wait_recv()
            d = dims[(k + j) % n]
            done = [dims[(k + i) % n] for i in range(j)]
            fixed = {m: bits[m] for m in LEAD if m not in done}
            fixed[d] = 1 - bits[d]
            piece = full.at[at(LEAD, fixed, cuts[k])]
            arriving.append(send.go(piece, piece, "core"))
    for c in arriving:
        c.wait_recv()


ICI3 = ("XA", "YA", "XB")
ICI4 = ("XA", "YA", "XB", "YB")


def landing(dims, width):
    n = len(dims)
    cuts = colours(n, width)
    return [
        pltpu.VMEM((2,) * (n - 1 - j) + (BLK, cuts[k][1]), jnp.bfloat16)
        for k in range(n)
        for j in range(n)
    ]


def forward_kernel(
    width, part, feats, gain, final_out, resid_out, scale_out,
    total, full, xown, send_sem, recv_sem, local_sem, *landed,
):
    bits, to = place()
    names = LEAD[1:]
    mine = at(names, bits)
    fetch = pltpu.make_async_copy(feats.at[mine], xown, local_sem.at[0])
    fetch.start()
    meet(to)
    send = Sender(send_sem, recv_sem, to)
    reduce_cube(send, bits, names, ICI3, width, part, total, landed)
    fetch.wait()
    hidden = total[at(ICI3, bits)].astype(jnp.float32)
    resid = xown[...].astype(jnp.float32) + hidden
    rscale = lax.rsqrt(jnp.mean(resid * resid, -1, keepdims=True) + EPS)
    resid_out[...] = resid
    scale_out[...] = jnp.broadcast_to(rscale, scale_out.shape)
    full[at(LEAD, bits)] = (resid * rscale * gain[...]).astype(jnp.bfloat16)
    gather_cube(send, bits, ICI4, width, full)
    put = pltpu.make_async_copy(full, final_out, local_sem.at[1])
    put.start()
    put.wait()
    send.drain()


def backward_kernel(
    width, run, part, resid, scale, gain, grad_own, grad_half,
    total, full, send_sem, recv_sem, local_sem, *landed,
):
    bits, to = place()
    runs = width // (2 * run)
    meet(to)
    send = Sender(send_sem, recv_sem, to)
    reduce_cube(send, bits, LEAD, ICI4, width, part, total, landed)
    rest = tuple(n for n in LEAD if n != "core")
    dfinal = total[at(rest, bits)].astype(jnp.float32)
    r = resid[...]
    rscale = scale[...][:, :1]
    scaled = dfinal * gain[...]
    inner = jnp.sum(scaled * r, -1, keepdims=True)
    full[at(LEAD, bits)] = (rscale * scaled - r * (rscale * rscale * rscale / width * inner)).astype(
        jnp.bfloat16
    )
    gather_cube(send, bits, ICI4, width, full)
    out = [
        pltpu.make_async_copy(full.at[at(LEAD, {"YB": bits["YB"]})], grad_own, local_sem.at[2 * runs])
    ]
    for b in range(runs):
        for s, slot in ((bits["YB"], 0), (1 - bits["YB"], 1)):
            col = pl.multiple_of((2 * b + bits["YB"]) * run, run)
            out.append(
                pltpu.make_async_copy(
                    full.at[at(LEAD, {"YB": s}, (col, run))],
                    grad_half.at[at(LEAD, {"YB": slot}, (b * run, run))],
                    local_sem.at[len(out) - 1],
                )
            )
    for c in out:
        c.start()
    for c in out:
        c.wait()
    send.drain()


def stats_kernel(stats, out, near, far, held, send_sem, recv_sem):
    x, ylo, yhi, core = (lax.axis_index(n) for n in ("x", "ylo", "yhi", "core"))
    row = [
        {"x": lax.rem(x + i, 4), "core": lax.rem(core + c, 2)}
        for i in range(4) for c in range(2) if i or c
    ]
    column = [
        {"ylo": lax.rem(ylo + a, 2), "yhi": lax.rem(yhi + b, 2)}
        for a in range(2) for b in range(2) if a or b
    ]
    barrier = pltpu.get_barrier_semaphore()
    for d in row + column:
        pl.semaphore_signal(barrier, inc=1, device_id=d, device_id_type=MESH)
    pl.semaphore_wait(barrier, len(row) + len(column))

    def exchange(src, slots, peers, base):
        flying = []
        for i, d in enumerate(peers):
            c = pltpu.make_async_remote_copy(
                src_ref=src,
                dst_ref=slots.at[i],
                send_sem=send_sem.at[base + i],
                recv_sem=recv_sem.at[base + i],
                device_id=d,
                device_id_type=MESH,
            )
            c.start()
            flying.append(c)
        for c in flying:
            c.wait_recv()
        parts = [src[...]] + [slots[i] for i in range(len(peers))]
        tops = [p[0:2] for p in parts]
        top = functools.reduce(jnp.maximum, tops)
        total = functools.reduce(
            jnp.add, [p[2:4] * jnp.exp(t - top) for p, t in zip(parts, tops)]
        )
        return flying, top, total

    one, top, total = exchange(stats, near, row, 0)
    held[0:2] = top
    held[2:4] = total
    held[4:8] = jnp.zeros((4, held.shape[1]), jnp.float32)
    two, top, total = exchange(held, far, column, len(row))
    out[0:2] = top
    out[2:4] = total
    out[4:8] = jnp.zeros((4, out.shape[1]), jnp.float32)
    for c in one + two:
        c.wait_send()


VM = pl.BlockSpec(memory_space=pltpu.VMEM)
ANY = pl.BlockSpec(memory_space=pl.ANY)
CUBE = (2,) * 5


def params(cid):
    return pltpu.CompilerParams(
        collective_id=cid, has_side_effects=True, vmem_limit_bytes=40 * 1024 * 1024
    )


def call_forward(part, feats, gain):
    width = part.shape[1]
    sd = jax.ShapeDtypeStruct
    bf16, f32 = jnp.bfloat16, jnp.float32
    n_sem = 6 + 9 + 1 + 32
    final, resid, scale = pl.pallas_call(
        functools.partial(forward_kernel, width),
        out_shape=(
            sd(CUBE + (BLK, width), bf16),
            sd((BLK, width), f32),
            sd((BLK, 128), f32),
        ),
        in_specs=[VM, ANY, VM],
        out_specs=(ANY, VM, VM),
        scratch_shapes=[
            pltpu.VMEM((2,) * 3 + (BLK, width), bf16),
            pltpu.VMEM(CUBE + (BLK, width), bf16),
            pltpu.VMEM((BLK, width), bf16),
            pltpu.SemaphoreType.DMA((n_sem,)),
            pltpu.SemaphoreType.DMA((n_sem,)),
            pltpu.SemaphoreType.DMA((2,)),
        ]
        + landing(ICI3, width),
        compiler_params=params(1),
        cost_estimate=pl.CostEstimate(flops=10**6, bytes_accessed=10**8, transcendentals=0),
        name="forward_plane",
    )(part.reshape(CUBE[1:] + (BLK, width)), feats.reshape(CUBE[1:] + (BLK, width)), gain[None])
    return final.reshape(-1, width), resid, scale


def call_backward(part, resid, scale, gain, run):
    width = resid.shape[1]
    sd = jax.ShapeDtypeStruct
    bf16 = jnp.bfloat16
    n_sem = 8 + 16 + 1 + 32
    own, halves = pl.pallas_call(
        functools.partial(backward_kernel, width, run),
        out_shape=(
            sd(CUBE[1:] + (BLK, width), bf16),
            sd(CUBE + (BLK, width // 2), bf16),
        ),
        in_specs=[VM, VM, VM, VM],
        out_specs=(ANY, ANY),
        scratch_shapes=[
            pltpu.VMEM((2,) * 4 + (BLK, width), bf16),
            pltpu.VMEM(CUBE + (BLK, width), bf16),
            pltpu.SemaphoreType.DMA((n_sem,)),
            pltpu.SemaphoreType.DMA((n_sem,)),
            pltpu.SemaphoreType.DMA((1 + width // run,)),
        ]
        + landing(ICI4, width),
        compiler_params=params(3),
        cost_estimate=pl.CostEstimate(flops=10**6, bytes_accessed=10**8, transcendentals=0),
        name="backward_plane",
    )(part.reshape(CUBE + (BLK, width)), resid, scale, gain[None])
    return own.reshape(-1, width), halves.reshape(-1, width // 2)


def call_stats(stats):
    f32 = jnp.float32
    n = stats.shape[1]
    return pl.pallas_call(
        stats_kernel,
        out_shape=jax.ShapeDtypeStruct((8, n), f32),
        in_specs=[VM],
        out_specs=VM,
        scratch_shapes=[
            pltpu.VMEM((7, 8, n), f32),
            pltpu.VMEM((3, 8, n), f32),
            pltpu.VMEM((8, n), f32),
            pltpu.SemaphoreType.DMA((10,)),
            pltpu.SemaphoreType.DMA((10,)),
        ],
        compiler_params=params(2),
        name="softmax_stats",
    )(stats)


def body(
    features, token_ids, positions, target_buffer, norm_gain, final_gain, w_in, w_out, head_weight
):
    yhi = lax.axis_index("yhi")
    vocab = lax.axis_index(("ylo", "x", "core"))
    f32 = jnp.float32
    bf16 = jnp.bfloat16
    backward = (((1,), (1,)), ((), ()))
    contract = (((0,), (0,)), ((), ()))
    swap = functools.partial(lax.ppermute, axis_name="yhi", perm=[(0, 1), (1, 0)])
    gather = functools.partial(lax.all_gather, axis_name="z", axis=0, tiled=True)
    scatter = functools.partial(lax.psum_scatter, axis_name="z", scatter_dimension=0, tiled=True)

    def pick(array, axis, index):
        return lax.dynamic_index_in_dim(array, index, axis, keepdims=False)

    def in_order(own, pair):
        return jnp.where(yhi == 0, jnp.concatenate([own, pair], 0), jnp.concatenate([pair, own], 0))

    rows, cols = head_weight.shape
    hw = head_weight.reshape(rows, 8, 2, cols // 16)
    head_pair = swap(pick(hw, 2, 1 - yhi).reshape(rows, cols // 2))
    head = gather(in_order(pick(hw, 2, yhi).reshape(rows, cols // 2), head_pair))

    tok, width = features.shape
    xfloat = features.astype(f32)
    rinput = lax.rsqrt(jnp.mean(xfloat * xfloat, -1, keepdims=True) + EPS)
    normed = (xfloat * rinput * norm_gain).astype(bf16)
    pre = jnp.dot(normed, w_in, preferred_element_type=f32)
    act = jax.nn.silu(pre).astype(bf16)
    part = jnp.dot(act, w_out, preferred_element_type=f32).astype(bf16)
    final, resid, scale = call_forward(part, features, final_gain)

    split = normed.reshape(tok, 8, 2, rows)
    normed_own = pick(split, 2, yhi).reshape(tok, width // 2)
    normed_pair = swap(pick(split, 2, 1 - yhi).reshape(tok, width // 2))
    act_pair = swap(act)

    tw = target_buffer.shape[1]
    ordered = target_buffer[positions].reshape(8, -1, tw)
    target = lax.all_to_all(ordered, "z", split_axis=0, concat_axis=2, tiled=True)[0]
    toks = in_order(token_ids, swap(token_ids))

    final, normed_pair, act_pair, target, toks = lax.optimization_barrier(
        (final, normed_pair, act_pair, target, toks)
    )
    normed2 = jnp.concatenate([normed_own, normed_pair], 0)
    act2 = jnp.concatenate([act, act_pair], 0)

    logits = jnp.dot(final, head, preferred_element_type=f32)
    tfloat = target.astype(f32)
    top_q = jnp.max(logits, -1)
    top_p = jnp.max(tfloat, -1)
    qexp = jnp.exp(logits - top_q[:, None])
    pexp = jnp.exp(tfloat - top_p[:, None])
    zero = jnp.zeros_like(top_q)
    stats = jnp.stack([top_q, top_p, jnp.sum(qexp, -1), jnp.sum(pexp, -1), zero, zero, zero, zero])
    every = call_stats(stats)
    qprob = qexp * (jnp.exp(top_q - every[0]) / every[2])[:, None]
    pprob = pexp * (jnp.exp(top_p - every[1]) / every[3])[:, None]
    lane = jnp.arange(cols // 2, dtype=jnp.int32)
    columns_here = vocab * cols + (lane // tw) * (2 * tw) + yhi * tw + lane % tw
    onehot = (columns_here[None, :] == toks[:, None]).astype(f32)
    dlogits = (qprob - pprob + HARD * (qprob - onehot)).astype(bf16)

    gh = lax.dot_general(final, dlogits, contract, preferred_element_type=f32).astype(bf16)
    gh, dlogits = lax.optimization_barrier((gh, dlogits))
    gh = scatter(gh).reshape(2, rows, cols // 2)
    both = jnp.stack([pick(gh, 0, yhi), swap(pick(gh, 0, 1 - yhi))]).reshape(2, rows, 8, tw)
    both = jnp.where(yhi == 0, both, both[::-1])
    grad_head = both.transpose(1, 2, 0, 3).reshape(rows, cols).astype(f32)

    part = lax.dot_general(dlogits, head, backward, preferred_element_type=f32).astype(bf16)
    dresid, dresid2 = call_backward(part, resid, scale, final_gain, rows)

    dact = lax.dot_general(dresid, w_out, backward, preferred_element_type=f32)
    sig = jax.nn.sigmoid(pre)
    dpre = (dact * sig * (1.0 + pre * (1.0 - sig))).astype(bf16)
    dpre2 = jnp.concatenate([dpre, swap(dpre)], 0)
    gf = jnp.concatenate(
        [
            lax.dot_general(normed2, dpre2, contract, preferred_element_type=f32),
            lax.dot_general(dresid2, act2, contract, preferred_element_type=f32),
        ],
        1,
    ).astype(bf16)
    gf = scatter(gf).astype(f32)
    units = act.shape[1]
    return (grad_head, gf[:, :units], gf[:, units:].T)


def solution(mesh):
    names = ("ylo", "x", "core", "z", "yhi")
    fine = Mesh(mesh.devices.reshape(2, 4, 2, 8, 2), names)
    v = ("ylo", "x", "core")
    d = ("z", "yhi")
    return jax.shard_map(
        body,
        mesh=fine,
        in_specs=(
            P(d, None),
            P(d),
            P(),
            P(None, v + d),
            P(),
            P(),
            P(None, v),
            P(v, None),
            P(d, v),
        ),
        out_specs=(P(d, v), P(d, v), P(v, d)),
        check_vma=False,
    )
```

```python
import functools
import jax
import jax.numpy as jnp
from jax import lax
from jax.experimental import pallas as pl
from jax.experimental.pallas import tpu as pltpu
from jax.sharding import Mesh, PartitionSpec as P

EPS = 1e-05
HARD = 0.5
MESH = pl.DeviceIdType.MESH
LEAD = ("YB", "core", "XA", "YA", "XB")
REST = ("YB", "XA", "YA", "XB")
ICI3 = ("XA", "YA", "XB")
ICI4 = ("XA", "YA", "XB", "YB")
CUBE = (2,) * 5
BLK = 16
F32 = jnp.float32
BF16 = jnp.bfloat16


def place():
    x, ylo, yhi, core, z = (lax.axis_index(n) for n in ("x", "ylo", "yhi", "core", "z"))
    nz = lax.axis_size("z")
    y = 2 * yhi + ylo
    odd = lax.rem(x, 2)
    bits = {
        "core": core,
        "XA": lax.rem(lax.div(x + 1, 2), 2),
        "XB": lax.div(x, 2),
        "YA": lax.rem(lax.div(y + 1, 2), 2),
        "YB": yhi,
    }
    to = {
        "core": {"core": 1 - core},
        "XA": {"x": x + 1 - 2 * odd},
        "XB": {"x": lax.rem(x + 3 + 2 * odd, 4)},
        "YA": {"ylo": 1 - ylo},
        "YB": {"ylo": 1 - ylo, "yhi": 1 - yhi},
        "pair": {"yhi": 1 - yhi},
        "up": {"z": lax.rem(z + 1, nz)},
        "down": {"z": lax.rem(z + nz - 1, nz)},
    }
    for i in range(1, nz):
        to[i] = {"z": lax.rem(z + i, nz)}
    return bits, to, z, nz


def at(names, fixed, cols=None):
    where = tuple(fixed.get(n, slice(None)) for n in names)
    return where + (slice(None), slice(None) if cols is None else pl.ds(*cols))


def corners(names):
    out = [{}]
    for n in names:
        out = [dict(o, **{n: v}) for o in out for v in (0, 1)]
    return out


class Sender:
    def __init__(self, send_sem, recv_sem, to):
        self.send_sem, self.recv_sem, self.to = send_sem, recv_sem, to
        self.all = []

    def go(self, src, dst, dim):
        n = len(self.all)
        c = pltpu.make_async_remote_copy(
            src_ref=src,
            dst_ref=dst,
            send_sem=self.send_sem.at[n],
            recv_sem=self.recv_sem.at[n],
            device_id=self.to[dim],
            device_id_type=MESH,
        )
        c.start()
        self.all.append(c)
        return c

    def drain(self):
        for c in self.all:
            c.wait_send()


class Local:
    def __init__(self, sem):
        self.sem = sem
        self.n = 0

    def go(self, src, dst):
        c = pltpu.make_async_copy(src, dst, self.sem.at[self.n])
        c.start()
        self.n += 1
        return c


def colours(n, width):
    tiles = width // 128
    edges = [128 * (tiles * k // n) for k in range(n + 1)]
    return [(edges[k], edges[k + 1] - edges[k]) for k in range(n)]


def meet(to, dims):
    barrier = pltpu.get_barrier_semaphore()
    for d in dims:
        pl.semaphore_signal(barrier, inc=1, device_id=to[d], device_id_type=MESH)
    pl.semaphore_wait(barrier, len(dims))


def step(thread):
    return next(thread, None)


def finish(thread):
    for _ in thread:
        pass


def reduce_cube(send, bits, names, dims, width, part, total, landed):
    rest = tuple(n for n in names if n != "core")
    n = len(dims)
    cuts = colours(n, width)
    first, second = [], []
    for keep, held in ((1, first), (0, second)):
        for k in range(n):
            d = dims[k]
            bit = 1 - bits[d] if keep else bits[d]
            src = part.at[at(names, {"core": 1 - bits["core"], d: bit}, cuts[k])]
            dst = total.at[at(rest, {d: bit}, cuts[k])]
            held.append(send.go(src, dst, "core"))

    def merge(k, bit):
        d = dims[k]
        for f in corners([m for m in rest if m != d]):
            f = dict(f, **{d: bit})
            w = at(rest, f, cuts[k])
            total[w] = total[w] + part[at(names, dict(f, core=bits["core"]), cuts[k])]

    def start(k, j):
        d = dims[(k + j) % n]
        fixed = {dims[(k + i) % n]: bits[dims[(k + i) % n]] for i in range(j)}
        fixed[d] = 1 - bits[d]
        return send.go(total.at[at(rest, fixed, cuts[k])], landed[k * n + j], d)

    yield
    flying = []
    for k in range(n):
        first[k].wait_recv()
        merge(k, 1 - bits[dims[k]])
        flying.append(start(k, 0))
    yield
    for k in range(n):
        second[k].wait_recv()
        merge(k, bits[dims[k]])
    for j in range(n):
        yield
        for k in range(n):
            flying[k].wait_recv()
            done = [dims[(k + i) % n] for i in range(j + 1)]
            fixed = {m: bits[m] for m in done}
            left = [m for m in rest if m not in done]
            for f in corners(left):
                w = at(rest, dict(f, **fixed), cuts[k])
                total[w] = total[w] + landed[k * n + j][tuple(f[m] for m in left)]
            if j + 1 < n:
                flying[k] = start(k, j + 1)


def gather_cube(send, bits, dims, width, full):
    n = len(dims)
    cuts = colours(n, width)
    arriving = []
    for j in range(n):
        flying = []
        for k in range(n):
            d = dims[(k + j) % n]
            done = [dims[(k + i) % n] for i in range(j)]
            piece = full.at[at(LEAD, {m: bits[m] for m in LEAD if m not in done}, cuts[k])]
            flying.append(send.go(piece, piece, d))
        if j == 0:
            arriving.append(send.go(full.at[at(LEAD, bits)], full.at[at(LEAD, bits)], "core"))
        yield
        for k in range(n):
            flying[k].wait_recv()
            d = dims[(k + j) % n]
            done = [dims[(k + i) % n] for i in range(j)]
            fixed = {m: bits[m] for m in LEAD if m not in done}
            fixed[d] = 1 - bits[d]
            piece = full.at[at(LEAD, fixed, cuts[k])]
            arriving.append(send.go(piece, piece, "core"))
    for c in arriving:
        c.wait_recv()


def ring_gather(send, z, nz, slots, full, late):
    half = nz // 2

    def block(i, q):
        return full.at[lax.rem(z + nz + i, nz), slots[q]]

    ups, downs = [None, None], [None, None]
    for q in range(2):
        if q:
            late.wait_recv()
        if half > 1 or q == 0:
            ups[q] = send.go(block(0, q), block(0, q), "up")
        if half > 1 or q == 1:
            downs[q] = send.go(block(0, q), block(0, q), "down")
        yield
    for s in range(1, half + 1):
        for q in range(2):
            if s < half or q == 0:
                ups[q].wait_recv()
                if s + 1 < half or (s + 1 == half and q == 0):
                    ups[q] = send.go(block(-s, q), block(-s, q), "up")
            if s < half or q == 1:
                downs[q].wait_recv()
                if s + 1 < half or (s + 1 == half and q == 1):
                    downs[q] = send.go(block(s, q), block(s, q), "down")
            yield


def ring_scatter(send, z, nz, part, ups, downs):
    half = nz // 2
    rows = part.shape[1] // 2
    cut = [pl.ds(0, rows), pl.ds(rows, rows)]

    def mine(i, q):
        return part.at[lax.rem(z + nz + i, nz), cut[q]]

    flying = {}
    for way, landed, sign, q in (("up", ups, 1, 0), ("down", downs, -1, 1)):
        flying[way, 0, q] = send.go(mine(sign * half, q), landed[0].at[cut[q]], way)
        if half > 1:
            q = 1 - q
            flying[way, 1, q] = send.go(mine(sign * (half - 1), q), landed[1].at[cut[q]], way)
    yield
    order = [(0, 0)] + [(s, q) for s in range(1, half) for q in (1, 0)]
    for s, lead in order:
        for way, landed, sign in (("up", ups, 1), ("down", downs, -1)):
            q = lead if way == "up" else 1 - lead
            flying[way, s, q].wait_recv()
            if s + 1 < half:
                ref = landed[s].at[cut[q]]
                ref[...] = ref[...] + mine(sign * (half - 1 - s), q)[...]
                flying[way, s + 1, q] = send.go(ref, landed[s + 1].at[cut[q]], way)
        yield


def ring_result(z, part, ups, downs):
    own = part[z].astype(F32)
    if len(ups) > 1:
        return own + ups[-1][...].astype(F32) + downs[-1][...].astype(F32)
    rows = part.shape[1] // 2
    return own + jnp.concatenate([ups[0][:rows], downs[0][rows:]], 0).astype(F32)


def landing(dims, width):
    n = len(dims)
    cuts = colours(n, width)
    return [
        pltpu.VMEM((2,) * (n - 1 - j) + (BLK, cuts[k][1]), BF16) for k in range(n) for j in range(n)
    ]


def forward_kernel(
    feats, gain_in, w_in, w_out, gain, hw, buf, pos, toks,
    final_out, head_out, resid_out, scale_out, normed_out, pre_out, target_out, toks_out,
    fv, w1, w2, bv, pv, normed, pre, part, total, full, head, ordered, target,
    send_sem, recv_sem, local_sem, *landed,
):
    bits, to, z, nz = place()
    yhi = bits["YB"]
    width = fv.shape[1]
    tok = fv.shape[0]
    run = head.shape[2]
    units = pre.shape[1]
    local = Local(local_sem)
    got_head = local.go(hw.at[yhi], head.at[z, yhi])
    got_f = local.go(feats, fv)
    got_w1 = local.go(w_in, w1)
    got_w2 = local.go(w_out, w2)
    got_p = local.go(pos, pv)
    got_b = local.go(buf, bv)
    meet(to, LEAD + ("pair", "up", "down") + tuple(range(2, nz - 1)))
    send = Sender(send_sem, recv_sem, to)
    late = send.go(hw.at[1 - yhi], head.at[z, yhi], "pair")
    got_head.wait()
    ring = ring_gather(send, z, nz, (yhi, 1 - yhi), head, late)
    step(ring)
    swapped = [send.go(toks, toks_out.at[yhi], "pair")]
    kept = [local.go(toks, toks_out.at[yhi])]

    got_f.wait()
    chunk = 32

    def norm_rows(i, _):
        rows = pl.ds(pl.multiple_of(i * chunk, chunk), chunk)
        x = fv[rows, :].astype(F32)
        r = lax.rsqrt(jnp.mean(x * x, -1, keepdims=True) + EPS)
        normed[rows, :] = (x * r * gain_in[...]).astype(BF16)
        return 0

    lax.fori_loop(0, tok // chunk, norm_rows, 0)
    for b in range(width // (2 * run)):
        there = pl.multiple_of((2 * b + 1 - yhi) * run, run)
        here = pl.multiple_of((2 * b + yhi) * run, run)
        cols = pl.ds(b * run, run)
        swapped.append(
            send.go(normed.at[:, pl.ds(there, run)], normed_out.at[yhi, :, cols], "pair")
        )
        kept.append(local.go(normed.at[:, pl.ds(here, run)], normed_out.at[yhi, :, cols]))
    got_w1.wait()
    deep = width // 4
    for c in range(4):
        k = pl.ds(c * deep, deep)
        prod = jnp.dot(normed[:, k], w1[k, :], preferred_element_type=F32)
        pre[...] = prod if c == 0 else pre[...] + prod
    swapped.append(send.go(pre, pre_out.at[yhi], "pair"))
    kept.append(local.go(pre, pre_out.at[yhi]))
    step(ring)
    v = pre[...]
    act = (v * jax.nn.sigmoid(v)).astype(BF16)
    got_w2.wait()
    wide = width // 8
    names = LEAD[1:]
    for c in range(8):
        cols = (c * wide, wide)
        block = jnp.dot(act, w2[:, pl.ds(*cols)], preferred_element_type=F32).astype(BF16)
        for i, f in enumerate(corners(names)):
            part[at(names, f, cols)] = block[i * BLK : (i + 1) * BLK]

    got_p.wait()
    got_b.wait()
    n_buf = bv.shape[0]
    piece = 512 if n_buf % 512 == 0 else n_buf

    def ordered_rows(i):
        dest = lax.rem(z + i, nz)

        def inner(t, sums):
            start = pl.multiple_of(t * piece, piece)
            rows = bv[pl.ds(start, piece), :]
            out = []
            for h in range(2):
                there = pv[dest, h] - start
                lane = lax.broadcasted_iota(jnp.int32, (tok, piece), 1)
                hot = jnp.where(there == lane, 1.0, 0.0).astype(BF16)
                out.append(sums[h] + jnp.dot(hot, rows, preferred_element_type=F32))
            return tuple(out)

        zero = jnp.zeros((tok, bv.shape[1]), F32)
        a, b = lax.fori_loop(0, n_buf // piece, inner, (zero, zero))
        return jnp.concatenate([a, b], 1).astype(BF16)

    def gather_target():
        for i in range(1, nz):
            ordered[i] = ordered_rows(i)
            way = "up" if i == 1 else "down" if i == nz - 1 else i
            swapped.append(send.go(ordered.at[i], target.at[z], way))
            yield
        target[z] = ordered_rows(0)
        yield

    rows16 = fv.at[pl.ds(pl.multiple_of(own_row(bits), BLK), BLK)]
    side = gather_target()
    for _ in reduce_cube(send, bits, names, ICI3, width, part, total, landed):
        step(side)
        step(ring)
    hidden = total[at(ICI3, bits)].astype(F32)
    resid = rows16[...].astype(F32) + hidden
    rscale = lax.rsqrt(jnp.mean(resid * resid, -1, keepdims=True) + EPS)
    resid_out[...] = resid
    scale_out[...] = jnp.broadcast_to(rscale, scale_out.shape)
    full[at(LEAD, bits)] = (resid * rscale * gain[...]).astype(BF16)
    for _ in gather_cube(send, bits, ICI4, width, full):
        step(side)
        step(ring)
    put = [local.go(full, final_out)]
    finish(side)
    finish(ring)
    put.append(local.go(head, head_out))
    for c in swapped:
        c.wait_recv()
    put.append(local.go(target, target_out))
    for c in kept + put:
        c.wait()
    send.drain()


def own_row(bits):
    r = bits["core"]
    for n in ("XA", "YA", "XB"):
        r = 2 * r + bits[n]
    return r * BLK


def backward_kernel(
    run, part, resid, scale, gain, gh, dresid_out, half_out, gh_out,
    total, full, gh_sum, send_sem, recv_sem, local_sem, *landed,
):
    bits, to, z, nz = place()
    width = part.shape[-1]
    h = nz // 2
    landed, ups, downs = landed[: -2 * h], landed[-2 * h : -h], landed[-h:]
    meet(to, LEAD + ("up", "down"))
    send = Sender(send_sem, recv_sem, to)
    local = Local(local_sem)
    ring = ring_scatter(send, z, nz, gh, ups, downs)
    step(ring)
    for i, _ in enumerate(reduce_cube(send, bits, LEAD, ICI4, width, part, total, landed)):
        if i >= 2:
            step(ring)
    dfinal = total[at(REST, bits)].astype(F32)
    r = resid[...]
    rscale = scale[...][:, :1]
    scaled = dfinal * gain[...]
    inner = jnp.sum(scaled * r, -1, keepdims=True)
    full[at(LEAD, bits)] = (rscale * scaled - r * (rscale * rscale * rscale / width * inner)).astype(
        BF16
    )
    for i, _ in enumerate(gather_cube(send, bits, ICI4, width, full)):
        step(ring)
    put = [local.go(full, dresid_out)]
    for b in range(width // (2 * run)):
        col = pl.multiple_of((2 * b + bits["YB"]) * run, run)
        put.append(local.go(full.at[at(LEAD, {}, (col, run))], half_out.at[at(LEAD, {}, (b * run, run))]))
    finish(ring)
    gh_sum[...] = ring_result(z, gh, ups, downs).astype(BF16)
    put.append(local.go(gh_sum, gh_out))
    for c in put:
        c.wait()
    send.drain()


def finish_kernel(gf, gh, gi_out, go_out, gh_out, send_sem, recv_sem, local_sem, *landed):
    bits, to, z, nz = place()
    yhi = bits["YB"]
    h = nz // 2
    ups, downs = landed[:h], landed[h:]
    meet(to, ("pair", "up", "down"))
    send = Sender(send_sem, recv_sem, to)
    ring = ring_scatter(send, z, nz, gf, ups, downs)
    step(ring)
    cross = send.go(gh.at[1 - yhi], gh_out.at[yhi], "pair")
    kept = pltpu.make_async_copy(gh.at[yhi], gh_out.at[yhi], local_sem.at[0])
    kept.start()
    finish(ring)
    total = ring_result(z, gf, ups, downs)
    units = gi_out.shape[1]
    gi_out[...] = total[:, :units]
    go_out[...] = total[:, units:]
    cross.wait_recv()
    kept.wait()
    send.drain()


def stats_kernel(stats, out, near, far, held, send_sem, recv_sem):
    x, ylo, yhi, core = (lax.axis_index(n) for n in ("x", "ylo", "yhi", "core"))
    row = [
        {"x": lax.rem(x + i, 4), "core": lax.rem(core + c, 2)}
        for i in range(4) for c in range(2) if i or c
    ]
    column = [
        {"ylo": lax.rem(ylo + a, 2), "yhi": lax.rem(yhi + b, 2)}
        for a in range(2) for b in range(2) if a or b
    ]
    barrier = pltpu.get_barrier_semaphore()
    for d in row + column:
        pl.semaphore_signal(barrier, inc=1, device_id=d, device_id_type=MESH)
    pl.semaphore_wait(barrier, len(row) + len(column))

    def exchange(src, slots, peers, base):
        flying = []
        for i, d in enumerate(peers):
            c = pltpu.make_async_remote_copy(
                src_ref=src,
                dst_ref=slots.at[i],
                send_sem=send_sem.at[base + i],
                recv_sem=recv_sem.at[base + i],
                device_id=d,
                device_id_type=MESH,
            )
            c.start()
            flying.append(c)
        for c in flying:
            c.wait_recv()
        parts = [src[...]] + [slots[i] for i in range(len(peers))]
        tops = [p[0:2] for p in parts]
        top = functools.reduce(jnp.maximum, tops)
        total = functools.reduce(
            jnp.add, [p[2:4] * jnp.exp(t - top) for p, t in zip(parts, tops)]
        )
        return flying, top, total

    one, top, total = exchange(stats, near, row, 0)
    held[0:2] = top
    held[2:4] = total
    held[4:8] = jnp.zeros((4, held.shape[1]), F32)
    two, top, total = exchange(held, far, column, len(row))
    out[0:2] = top
    out[2:4] = total
    out[4:8] = jnp.zeros((4, out.shape[1]), F32)
    for c in one + two:
        c.wait_send()


VM = pl.BlockSpec(memory_space=pltpu.VMEM)
ANY = pl.BlockSpec(memory_space=pl.ANY)
SD = jax.ShapeDtypeStruct


def params(cid):
    return pltpu.CompilerParams(
        collective_id=cid, has_side_effects=True, vmem_limit_bytes=56 * 1024 * 1024
    )


def sems(remote, local):
    dma = pltpu.SemaphoreType.DMA
    return [dma((remote,)), dma((remote,)), dma((local,))]


def call_forward(feats, gain_in, w_in, w_out, gain, hw, buf, pos, toks):
    tok, width = feats.shape
    units = w_in.shape[1]
    _, rows, cols = hw.shape
    nz = lax.axis_size("z")
    tw = buf.shape[1]
    scratch = [
        pltpu.VMEM((tok, width), BF16),
        pltpu.VMEM((width, units), BF16),
        pltpu.VMEM((units, width), BF16),
        pltpu.VMEM(buf.shape, BF16),
        pltpu.VMEM(pos.shape, jnp.int32),
        pltpu.VMEM((tok, width), BF16),
        pltpu.VMEM((tok, units), F32),
        pltpu.VMEM(CUBE[1:] + (BLK, width), BF16),
        pltpu.VMEM(CUBE[2:] + (BLK, width), BF16),
        pltpu.VMEM(CUBE + (BLK, width), BF16),
        pltpu.VMEM((nz, 2, rows, cols), BF16),
        pltpu.VMEM((nz, tok, 2 * tw), BF16),
        pltpu.VMEM((nz, tok, 2 * tw), BF16),
    ]
    return pl.pallas_call(
        forward_kernel,
        out_shape=(
            SD(CUBE + (BLK, width), BF16),
            SD((nz, 2, rows, cols), BF16),
            SD((BLK, width), F32),
            SD((BLK, 128), F32),
            SD((2, tok, width // 2), BF16),
            SD((2, tok, units), F32),
            SD((nz, tok, 2 * tw), BF16),
            SD((2,) + toks.shape, jnp.int32),
        ),
        in_specs=[ANY, VM, ANY, ANY, VM, ANY, ANY, ANY, ANY],
        out_specs=(ANY, ANY, VM, VM, ANY, ANY, ANY, ANY),
        scratch_shapes=scratch + sems(96, 48) + landing(ICI3, width),
        compiler_params=params(1),
        cost_estimate=pl.CostEstimate(flops=10**10, bytes_accessed=10**8, transcendentals=0),
        name="forward_plane",
    )(feats, gain_in[None], w_in, w_out, gain[None], hw, buf, pos, toks)


def call_backward(part, resid, scale, gain, gh, run):
    width = resid.shape[1]
    nz, rows, cols = gh.shape
    ring = [pltpu.VMEM((rows, cols), BF16) for _ in range(nz)]
    return pl.pallas_call(
        functools.partial(backward_kernel, run),
        out_shape=(
            SD(CUBE + (BLK, width), BF16),
            SD(CUBE + (BLK, width // 2), BF16),
            SD((rows, cols), BF16),
        ),
        in_specs=[VM] * 5,
        out_specs=(ANY, ANY, ANY),
        scratch_shapes=[
            pltpu.VMEM((2,) * 4 + (BLK, width), BF16),
            pltpu.VMEM(CUBE + (BLK, width), BF16),
            pltpu.VMEM((rows, cols), BF16),
        ]
        + sems(80, 2 + width // run)
        + landing(ICI4, width)
        + ring,
        compiler_params=params(3),
        cost_estimate=pl.CostEstimate(flops=10**6, bytes_accessed=10**8, transcendentals=0),
        name="backward_plane",
    )(part.reshape(CUBE + (BLK, width)), resid, scale, gain[None], gh)


def call_finish(gf, gh):
    nz, rows, cols = gf.shape
    return pl.pallas_call(
        finish_kernel,
        out_shape=(SD((rows, cols // 2), F32), SD((rows, cols // 2), F32), SD(gh.shape, BF16)),
        in_specs=[VM, ANY],
        out_specs=(VM, VM, ANY),
        scratch_shapes=sems(24, 1) + [pltpu.VMEM((rows, cols), BF16) for _ in range(nz)],
        compiler_params=params(4),
        name="finish_ring",
    )(gf, gh)


def call_stats(stats):
    n = stats.shape[1]
    return pl.pallas_call(
        stats_kernel,
        out_shape=SD((8, n), F32),
        in_specs=[VM],
        out_specs=VM,
        scratch_shapes=[
            pltpu.VMEM((7, 8, n), F32),
            pltpu.VMEM((3, 8, n), F32),
            pltpu.VMEM((8, n), F32),
            pltpu.SemaphoreType.DMA((10,)),
            pltpu.SemaphoreType.DMA((10,)),
        ],
        compiler_params=params(2),
        name="softmax_stats",
    )(stats)


def body(
    features, token_ids, positions, target_buffer, norm_gain, final_gain, w_in, w_out, head_weight
):
    yhi = lax.axis_index("yhi")
    vocab = lax.axis_index(("ylo", "x", "core"))
    nz = lax.axis_size("z")
    backward = (((1,), (1,)), ((), ()))
    contract = (((0,), (0,)), ((), ()))
    rows, cols = head_weight.shape
    tok, width = features.shape
    units = w_in.shape[1]
    tw = target_buffer.shape[1]

    hw = head_weight.reshape(rows, nz, 2, tw).transpose(2, 0, 1, 3).reshape(2, rows, cols // 2)
    pos = positions.reshape(nz, 2, tok, 1)
    toks = jnp.zeros((8, 128), jnp.int32).at[: tok // 128].set(token_ids.reshape(tok // 128, 128))
    final, head, resid, scale, normed, pre, target, toks = call_forward(
        features, norm_gain, w_in, w_out, final_gain, hw, target_buffer, pos, toks
    )
    final = final.reshape(2 * tok, width)
    head = head.reshape(width, cols // 2)
    normed = normed.reshape(2 * tok, width // 2)
    pre = pre.reshape(2 * tok, units)
    target = target.reshape(nz, tok, 2, tw).transpose(2, 1, 0, 3).reshape(2 * tok, cols // 2)
    toks = toks[:, : tok // 128].reshape(2 * tok)

    logits = jnp.dot(final, head, preferred_element_type=F32)
    tfloat = target.astype(F32)
    top_q = jnp.max(logits, -1)
    top_p = jnp.max(tfloat, -1)
    qexp = jnp.exp(logits - top_q[:, None])
    pexp = jnp.exp(tfloat - top_p[:, None])
    zero = jnp.zeros_like(top_q)
    stats = jnp.stack([top_q, top_p, jnp.sum(qexp, -1), jnp.sum(pexp, -1), zero, zero, zero, zero])
    every = call_stats(stats)
    qprob = qexp * (jnp.exp(top_q - every[0]) / every[2])[:, None]
    pprob = pexp * (jnp.exp(top_p - every[1]) / every[3])[:, None]
    lane = jnp.arange(cols // 2, dtype=jnp.int32)
    columns_here = vocab * cols + (lane // tw) * (2 * tw) + yhi * tw + lane % tw
    onehot = (columns_here[None, :] == toks[:, None]).astype(F32)
    dlogits = (qprob - pprob + HARD * (qprob - onehot)).astype(BF16)

    gh = lax.dot_general(final, dlogits, contract, preferred_element_type=F32).astype(BF16)
    part = lax.dot_general(dlogits, head, backward, preferred_element_type=F32).astype(BF16)
    dresid, dresid_half, gh = call_backward(
        part, resid, scale, final_gain, gh.reshape(nz, 2 * rows, cols // 2), rows
    )
    dresid = dresid.reshape(2 * tok, width)
    dresid_half = dresid_half.reshape(2 * tok, width // 2)

    sig = jax.nn.sigmoid(pre)
    act = (pre * sig).astype(BF16)
    dact = lax.dot_general(dresid, w_out, backward, preferred_element_type=F32)
    dpre = (dact * sig * (1.0 + pre * (1.0 - sig))).astype(BF16)
    gf = jnp.concatenate(
        [
            lax.dot_general(normed, dpre, contract, preferred_element_type=F32),
            lax.dot_general(dresid_half, act, contract, preferred_element_type=F32),
        ],
        1,
    ).astype(BF16)
    gi, go, gh = call_finish(
        gf.reshape(nz, rows, 2 * units), gh.reshape(2, rows, cols // 2)
    )
    gh = gh.reshape(2, rows, nz, tw).transpose(1, 2, 0, 3).reshape(rows, cols).astype(F32)
    return (gh, gi, go.T)


def solution(mesh):
    names = ("ylo", "x", "core", "z", "yhi")
    fine = Mesh(mesh.devices.reshape(2, 4, 2, -1, 2), names)
    v = ("ylo", "x", "core")
    d = ("z", "yhi")
    return jax.shard_map(
        body,
        mesh=fine,
        in_specs=(
            P(d, None),
            P(d),
            P(),
            P(None, v + d),
            P(),
            P(),
            P(None, v),
            P(v, None),
            P(d, v),
        ),
        out_specs=(P(d, v), P(d, v), P(v, d)),
        check_vma=False,
    )
```

```python
import functools
import jax
import jax.numpy as jnp
from jax import lax
from jax.experimental import pallas as pl
from jax.experimental.pallas import tpu as pltpu
from jax.sharding import Mesh, PartitionSpec as P

EPS = 1e-05
HARD = 0.5
MESH = pl.DeviceIdType.MESH
LEAD = ("YB", "core", "XA", "YA", "XB")
REST = ("YB", "XA", "YA", "XB")
ICI3 = ("XA", "YA", "XB")
ICI4 = ("XA", "YA", "XB", "YB")
CUBE = (2,) * 5
BLK = 16
F32 = jnp.float32
BF16 = jnp.bfloat16


SCHED = ((1, 2, 4), (1, 2, 3), (0, 2, 4, 5), (0, 1, 2, 3))


def place():
    x, ylo, yhi, core, z = (lax.axis_index(n) for n in ("x", "ylo", "yhi", "core", "z"))
    nz = lax.axis_size("z")
    y = 2 * yhi + ylo
    odd = lax.rem(x, 2)
    bits = {
        "core": core,
        "XA": lax.rem(lax.div(x + 1, 2), 2),
        "XB": lax.div(x, 2),
        "YA": lax.rem(lax.div(y + 1, 2), 2),
        "YB": yhi,
    }
    to = {
        "core": {"core": 1 - core},
        "XA": {"x": x + 1 - 2 * odd},
        "XB": {"x": lax.rem(x + 3 + 2 * odd, 4)},
        "YA": {"ylo": 1 - ylo},
        "YB": {"ylo": 1 - ylo, "yhi": 1 - yhi},
        "pair": {"yhi": 1 - yhi},
        "up": {"z": lax.rem(z + 1, nz)},
        "down": {"z": lax.rem(z + nz - 1, nz)},
    }
    for i in range(1, nz):
        to[i] = {"z": lax.rem(z + i, nz)}
    for i in range(4):
        for c in range(2):
            to["row", i, c] = {"x": lax.rem(x + i, 4), "core": lax.rem(core + c, 2)}
    for a in range(2):
        for b in range(2):
            to["col", a, b] = {"ylo": lax.rem(ylo + a, 2), "yhi": lax.rem(yhi + b, 2)}
    return bits, to, z, nz


def at(names, fixed, cols=None):
    where = tuple(fixed.get(n, slice(None)) for n in names)
    return where + (slice(None), slice(None) if cols is None else pl.ds(*cols))


def corners(names):
    out = [{}]
    for n in names:
        out = [dict(o, **{n: v}) for o in out for v in (0, 1)]
    return out


class Sender:
    def __init__(self, send_sem, recv_sem, to):
        self.send_sem, self.recv_sem, self.to = send_sem, recv_sem, to
        self.all = []

    def go(self, src, dst, dim):
        n = len(self.all)
        c = pltpu.make_async_remote_copy(
            src_ref=src,
            dst_ref=dst,
            send_sem=self.send_sem.at[n],
            recv_sem=self.recv_sem.at[n],
            device_id=self.to[dim],
            device_id_type=MESH,
        )
        c.start()
        self.all.append(c)
        return c

    def drain(self):
        for c in self.all:
            c.wait_send()


class Local:
    def __init__(self, sem):
        self.sem = sem
        self.n = 0

    def go(self, src, dst):
        c = pltpu.make_async_copy(src, dst, self.sem.at[self.n])
        c.start()
        self.n += 1
        return c


def colours(n, width):
    tiles = width // 128
    edges = [128 * (tiles * k // n) for k in range(n + 1)]
    return [(edges[k], edges[k + 1] - edges[k]) for k in range(n)]


def greet(to, dims):
    barrier = pltpu.get_barrier_semaphore()
    for d in dims:
        pl.semaphore_signal(barrier, inc=1, device_id=to[d], device_id_type=MESH)
    return lambda: pl.semaphore_wait(barrier, len(dims))


def meet(to, dims):
    greet(to, dims)()


def step(thread):
    return next(thread, None)


def finish(thread):
    for _ in thread:
        pass


def reduce_cube(send, bits, names, dims, width, part, total, landed):
    rest = tuple(n for n in names if n != "core")
    n = len(dims)
    cuts = colours(n, width)
    first, second = [], []
    for keep, held in ((1, first), (0, second)):
        for k in range(n):
            d = dims[k]
            bit = 1 - bits[d] if keep else bits[d]
            src = part.at[at(names, {"core": 1 - bits["core"], d: bit}, cuts[k])]
            dst = total.at[at(rest, {d: bit}, cuts[k])]
            held.append(send.go(src, dst, "core"))

    def merge(k, bit):
        d = dims[k]
        for f in corners([m for m in rest if m != d]):
            f = dict(f, **{d: bit})
            w = at(rest, f, cuts[k])
            total[w] = total[w] + part[at(names, dict(f, core=bits["core"]), cuts[k])]

    def start(k, j):
        d = dims[(k + j) % n]
        fixed = {dims[(k + i) % n]: bits[dims[(k + i) % n]] for i in range(j)}
        fixed[d] = 1 - bits[d]
        return send.go(total.at[at(rest, fixed, cuts[k])], landed[k * n + j], d)

    yield
    flying = []
    for k in range(n):
        first[k].wait_recv()
        merge(k, 1 - bits[dims[k]])
        flying.append(start(k, 0))
    yield
    for k in range(n):
        second[k].wait_recv()
        merge(k, bits[dims[k]])
    for j in range(n):
        yield
        for k in range(n):
            flying[k].wait_recv()
            done = [dims[(k + i) % n] for i in range(j + 1)]
            fixed = {m: bits[m] for m in done}
            left = [m for m in rest if m not in done]
            for f in corners(left):
                w = at(rest, dict(f, **fixed), cuts[k])
                total[w] = total[w] + landed[k * n + j][tuple(f[m] for m in left)]
            if j + 1 < n:
                flying[k] = start(k, j + 1)


def gather_cube(send, bits, dims, width, full, names=LEAD):
    n = len(dims)
    cuts = colours(n, width)
    arriving = []
    for j in range(n):
        flying = []
        for k in range(n):
            d = dims[(k + j) % n]
            done = [dims[(k + i) % n] for i in range(j)]
            piece = full.at[at(names, {m: bits[m] for m in names if m not in done}, cuts[k])]
            flying.append(send.go(piece, piece, d))
        if j == 0:
            arriving.append(send.go(full.at[at(names, bits)], full.at[at(names, bits)], "core"))
        yield
        for k in range(n):
            flying[k].wait_recv()
            d = dims[(k + j) % n]
            done = [dims[(k + i) % n] for i in range(j)]
            fixed = {m: bits[m] for m in names if m not in done}
            fixed[d] = 1 - bits[d]
            piece = full.at[at(names, fixed, cuts[k])]
            arriving.append(send.go(piece, piece, "core"))
    for c in arriving:
        c.wait_recv()


def ring_gather(send, z, nz, slots, full, late):
    half = nz // 2

    def block(i, q):
        return full.at[lax.rem(z + nz + i, nz), slots[q]]

    ups, downs = [None, None], [None, None]
    for q in range(2):
        if q:
            late.wait_recv()
        if half > 1 or q == 0:
            ups[q] = send.go(block(0, q), block(0, q), "up")
        if half > 1 or q == 1:
            downs[q] = send.go(block(0, q), block(0, q), "down")
        yield
    for s in range(1, half + 1):
        for q in range(2):
            if s < half or q == 0:
                ups[q].wait_recv()
                if s + 1 < half or (s + 1 == half and q == 0):
                    ups[q] = send.go(block(-s, q), block(-s, q), "up")
            if s < half or q == 1:
                downs[q].wait_recv()
                if s + 1 < half or (s + 1 == half and q == 1):
                    downs[q] = send.go(block(s, q), block(s, q), "down")
            yield


def ring_scatter(send, z, nz, part, ups, downs, prepare):
    half = nz // 2
    rows = part.shape[1] // 2
    cut = [pl.ds(0, rows), pl.ds(rows, rows)]

    def block(i):
        return lax.rem(z + nz + i, nz)

    def mine(i, q):
        return part.at[block(i), cut[q]]

    flying = {}
    ways = (("up", ups, 1), ("down", downs, -1))
    prepare(block(half))
    for way, landed, sign in ways:
        q = 0 if way == "up" else 1
        flying[way, 0, q] = send.go(mine(sign * half, q), landed[0].at[cut[q]], way)
    if half > 1:
        for way, landed, sign in ways:
            q = 1 if way == "up" else 0
            prepare(block(sign * (half - 1)))
            flying[way, 1, q] = send.go(mine(sign * (half - 1), q), landed[1].at[cut[q]], way)
    yield
    for s in range(half):
        if half - 1 - s > 0 and s > 0:
            prepare(block(half - 1 - s))
            prepare(block(s + 1 - half))
        elif s == half - 1:
            prepare(block(0))
        for lead in (1, 0) if s else (0,):
            for way, landed, sign in ways:
                q = lead if way == "up" else 1 - lead
                flying[way, s, q].wait_recv()
                if s + 1 < half:
                    ref = landed[s].at[cut[q]]
                    ref[...] = ref[...] + mine(sign * (half - 1 - s), q)[...]
                    flying[way, s + 1, q] = send.go(ref, landed[s + 1].at[cut[q]], way)
            yield


def ring_result(z, part, ups, downs):
    own = part[z].astype(F32)
    if len(ups) > 1:
        return own + ups[-1][...].astype(F32) + downs[-1][...].astype(F32)
    rows = part.shape[1] // 2
    return own + jnp.concatenate([ups[0][:rows], downs[0][rows:]], 0).astype(F32)


def landing(dims, width):
    n = len(dims)
    cuts = colours(n, width)
    return [
        pltpu.VMEM((2,) * (n - 1 - j) + (BLK, cuts[k][1]), BF16) for k in range(n) for j in range(n)
    ]


def forward_kernel(
    feats, gain_in, w_in, w_out, gain, hw, buf, pos, toks,
    final_out, head_out, resid_out, scale_out, normed_out, pre_out, target_out, toks_out,
    fv, w1, w2, bv, bn, normed, other, pre, part, total, full, head, ordered, target,
    send_sem, recv_sem, local_sem, *landed,
):
    bits, to, z, nz = place()
    yhi = bits["YB"]
    tok, width = fv.shape
    run = head.shape[2]
    names = LEAD[1:]
    greeted = greet(to, LEAD + ("pair", "up", "down") + tuple(range(2, nz - 1)))
    local = Local(local_sem)
    got_f = local.go(feats, fv)
    got_head = local.go(hw.at[yhi], head.at[z, yhi])
    got_w1 = local.go(w_in, w1)
    got_w2 = local.go(w_out, w2)
    got_b = local.go(buf, bv)
    got_f.wait()
    chunk = 64

    def norm_rows(i, _):
        rows = pl.ds(pl.multiple_of(i * chunk, chunk), chunk)
        x = fv[rows, :].astype(F32)
        r = lax.rsqrt(jnp.mean(x * x, -1, keepdims=True) + EPS)
        normed[rows, :] = (x * r * gain_in[...]).astype(BF16)
        return 0

    lax.fori_loop(0, tok // chunk, norm_rows, 0)
    greeted()
    send = Sender(send_sem, recv_sem, to)
    late = send.go(hw.at[1 - yhi], head.at[z, yhi], "pair")
    got_head.wait()
    ring = ring_gather(send, z, nz, (yhi, 1 - yhi), head, late)
    step(ring)
    swapped = [send.go(toks, toks_out.at[yhi], "pair")]
    kept = [local.go(toks, toks_out.at[yhi])]
    mine = pl.ds(pl.multiple_of(own_row(bits), BLK), BLK)
    crossed = send.go(normed.at[mine], other.at[at(names, bits)], "YB")

    def project(rows):
        deep = width // 4
        for c in range(4):
            k = pl.ds(c * deep, deep)
            prod = lax.dot_general(
                rows[:, k], w1[:, k], (((1,), (1,)), ((), ())), preferred_element_type=F32
            )
            pre[...] = prod if c == 0 else pre[...] + prod

    got_w1.wait()
    project(normed)
    pre_out[yhi] = pre[...]
    step(ring)
    v = pre[...]
    act = (v * jax.nn.sigmoid(v)).astype(BF16)
    got_w2.wait()
    wide = width // 8
    for c in range(8):
        cols = (c * wide, wide)
        block = jnp.dot(act, w2[:, pl.ds(*cols)], preferred_element_type=F32).astype(BF16)
        for i, f in enumerate(corners(names)):
            part[at(names, f, cols)] = block[i * BLK : (i + 1) * BLK]

    got_b.wait()
    n_buf = bv.shape[1]
    piece = 1024 if n_buf % 1024 == 0 else n_buf
    pos_t = pos[...].T

    def ordered_rows(i):
        dest = lax.rem(z + i, nz)
        lane = lax.broadcasted_iota(jnp.int32, pos_t.shape, 1)
        there = [
            jnp.sum(jnp.where(lane == 2 * dest + h, pos_t, 0.0), 1, keepdims=True) for h in range(2)
        ]
        cols = lax.broadcasted_iota(jnp.int32, (tok, piece), 1).astype(F32)

        def inner(t, sums):
            rows = bn[pl.ds(pl.multiple_of(t * piece, piece), piece), :]
            out = []
            for h in range(2):
                hot = jnp.where(there[h] - (t * piece).astype(F32) == cols, 1.0, 0.0).astype(BF16)
                out.append(sums[h] + jnp.dot(hot, rows, preferred_element_type=F32))
            return tuple(out)

        zero = jnp.zeros((tok, bv.shape[0]), F32)
        a, b = lax.fori_loop(0, n_buf // piece, inner, (zero, zero))
        return jnp.concatenate([a, b], 1).astype(BF16)

    def gather_target():
        for i in range(1, nz):
            ordered[i] = ordered_rows(i)
            way = "up" if i == 1 else "down" if i == nz - 1 else i
            swapped.append(send.go(ordered.at[i], target.at[z], way))
            yield
        target[z] = ordered_rows(0)
        yield

    def gather_other():
        crossed.wait_recv()
        yield from gather_cube(send, bits, ICI3, width, other, names)

    side = gather_target()
    cross = gather_other()
    for i, _ in enumerate(reduce_cube(send, bits, names, ICI3, width, part, total, landed)):
        if i == 0:
            bn[...] = bv[...].T
        step(side)
        if i in SCHED[0]:
            step(ring)
        if i >= 1:
            step(cross)
    hidden = total[at(ICI3, bits)].astype(F32)
    resid = fv[mine, :].astype(F32) + hidden
    rscale = lax.rsqrt(jnp.mean(resid * resid, -1, keepdims=True) + EPS)
    resid_out[...] = resid
    scale_out[...] = jnp.broadcast_to(rscale, scale_out.shape)
    full[at(LEAD, bits)] = (resid * rscale * gain[...]).astype(BF16)
    for i, _ in enumerate(gather_cube(send, bits, ICI4, width, full)):
        step(side)
        if i in SCHED[1]:
            step(ring)
    put = [local.go(full, final_out)]
    finish(side)
    step(ring)
    finish(cross)
    for i, f in enumerate(corners(names)):
        fv[i * BLK : (i + 1) * BLK, :] = other[at(names, f)]
    for src, slot in ((normed, yhi), (fv, 1 - yhi)):
        for b in range(width // (2 * run)):
            here = pl.ds(pl.multiple_of((2 * b + yhi) * run, run), run)
            put.append(local.go(src.at[:, here], normed_out.at[slot, :, pl.ds(b * run, run)]))
    project(fv)
    pre_out[1 - yhi] = pre[...]
    finish(ring)
    put.append(local.go(head, head_out))
    for c in swapped:
        c.wait_recv()
    put.append(local.go(target, target_out))
    for c in kept + put:
        c.wait()
    send.drain()


def own_row(bits):
    r = bits["core"]
    for n in ("XA", "YA", "XB"):
        r = 2 * r + bits[n]
    return r * BLK


def exchange_stats(send, own, near, held, far, out):
    def merge(src, slots, peers, dst):
        flying = [send.go(src, slots.at[i], p) for i, p in enumerate(peers)]
        for c in flying:
            c.wait_recv()
        parts = [src[...]] + [slots[i] for i in range(len(peers))]
        tops = [p[0:2] for p in parts]
        top = functools.reduce(jnp.maximum, tops)
        total = functools.reduce(
            jnp.add, [p[2:4] * jnp.exp(t - top) for p, t in zip(parts, tops)]
        )
        dst[0:2] = top
        dst[2:4] = total

    held[4:8] = jnp.zeros((4, held.shape[1]), F32)
    merge(own, near, [("row", i, c) for i in range(4) for c in range(2) if i or c], held)
    merge(held, far, [("col", a, b) for a in range(2) for b in range(2) if a or b], out)


NT = (((1,), (1,)), ((), ()))
TN = (((0,), (0,)), ((), ()))


def backward_kernel(
    run, first_col, final, head, target, w_out, normed, pre, toks, resid, scale, gain,
    gh_out, gi_out, go_out,
    fin, hv, tv, w2, nv, pexp, lg, own, near, held, far, back, dl, part, total, full,
    ghp, ghs, ghx, ghv, gfp, da, act, dpre,
    send_sem, recv_sem, local_sem, *landed,
):
    bits, to, z, nz = place()
    yhi = bits["YB"]
    n_tok, width = fin.shape
    n_col = hv.shape[1]
    units = w2.shape[0]
    tok, tw = tv.shape[1], tv.shape[2] // 2
    h = nz // 2
    rings, landed = landed[: 4 * h], landed[4 * h :]
    peers = [("row", i, c) for i in range(4) for c in range(2) if i or c]
    peers += [("col", a, b) for a in range(2) for b in range(2) if a or b]
    greeted = greet(to, peers + ["up", "down"])
    local = Local(local_sem)
    got_t = local.go(target, tv)
    got_fin = local.go(final, fin)
    got_hv = local.go(head, hv)
    got_w2 = local.go(w_out, w2)
    got_nv = local.go(normed, nv)
    send = Sender(send_sem, recv_sem, to)

    got_t.wait()
    for k in range(nz // 2):
        for s in range(2):
            lanes = slice(s * tw, (s + 1) * tw)
            two = [tv[2 * k + i].astype(F32)[:, lanes] for i in range(2)]
            pexp[s * tok : (s + 1) * tok, k * 2 * tw : (k + 1) * 2 * tw] = jnp.concatenate(two, 1)
    t = pexp[...]
    top_p = jnp.max(t, -1, keepdims=True)
    t = jnp.exp(t - top_p)
    pexp[...] = t
    sum_p = jnp.sum(t, -1, keepdims=True)

    got_fin.wait()
    got_hv.wait()
    deep = width // 4
    for c in range(4):
        k = pl.ds(c * deep, deep)
        prod = jnp.dot(fin[:, k], hv[k, :], preferred_element_type=F32)
        lg[...] = prod if c == 0 else lg[...] + prod
    t = lg[...]
    top_q = jnp.max(t, -1, keepdims=True)
    t = jnp.exp(t - top_q)
    lg[...] = t
    sum_q = jnp.sum(t, -1, keepdims=True)
    lane = lax.broadcasted_iota(jnp.int32, (n_tok, 128), 1)
    columns = jnp.where(
        lane == 0, top_q, jnp.where(lane == 1, top_p, jnp.where(lane == 2, sum_q, sum_p))
    )
    own[...] = columns.T[0:8]
    greeted()
    back[...] = jnp.zeros(back.shape, F32)
    back[8:16] = toks[...]
    exchange_stats(send, own, near, held, far, back)
    columns = back[...].T
    all_q, all_p, tot_q, tot_p, token = (columns[:, i : i + 1] for i in (0, 1, 2, 3, 8))
    q = lg[...] * (jnp.exp(top_q - all_q) / tot_q)
    p = pexp[...] * (jnp.exp(top_p - all_p) / tot_p)
    lane = lax.broadcasted_iota(jnp.int32, (n_tok, n_col), 1)
    shift = tw.bit_length() - 1
    here = first_col() + lane + jnp.left_shift(jnp.right_shift(lane, shift), shift)
    onehot = jnp.where(token.astype(jnp.int32) == here, 1.0, 0.0)
    dl[...] = (q - p + HARD * (q - onehot)).astype(BF16)

    wide = width // 8
    for c in range(8):
        cols = (c * wide, wide)
        block = lax.dot_general(
            dl[...], hv[pl.ds(*cols), :], NT, preferred_element_type=F32
        ).astype(BF16)
        for i, f in enumerate(corners(LEAD)):
            part[at(LEAD, f, cols)] = block[i * BLK : (i + 1) * BLK]

    def make_gh(b):
        cols = pl.ds(pl.multiple_of(b * 2 * run, 2 * run), 2 * run)
        ghp[b] = lax.dot_general(dl[...], fin[:, cols], TN, preferred_element_type=F32).astype(BF16)

    ring = ring_scatter(send, z, nz, ghp, rings[:h], rings[h : 2 * h], make_gh)
    for i, _ in enumerate(reduce_cube(send, bits, LEAD, ICI4, width, part, total, landed)):
        if i in SCHED[2]:
            step(ring)
    dfinal = total[at(REST, bits)].astype(F32)
    r = resid[...]
    rscale = scale[...][:, :1]
    scaled = dfinal * gain[...]
    inner = jnp.sum(scaled * r, -1, keepdims=True)
    full[at(LEAD, bits)] = (rscale * scaled - r * (rscale * rscale * rscale / width * inner)).astype(
        BF16
    )
    for i, _ in enumerate(gather_cube(send, bits, ICI4, width, full)):
        if i in SCHED[3]:
            step(ring)

    def dresid(start, size):
        return full[at(LEAD, {}, (start, size))].reshape(n_tok, size)

    got_w2.wait()
    for c in range(4):
        k = pl.ds(c * deep, deep)
        prod = lax.dot_general(dresid(c * deep, deep), w2[:, k], NT, preferred_element_type=F32)
        da[...] = prod if c == 0 else da[...] + prod
    v = pre[...]
    sig = jax.nn.sigmoid(v)
    act[...] = (v * sig).astype(BF16)
    dpre[...] = (da[...] * sig * (1.0 + v * (1.0 - sig))).astype(BF16)
    got_nv.wait()

    def make_gf(b):
        cols = pl.ds(pl.multiple_of(b * run, run), run)
        gfp[b, 0:units] = lax.dot_general(
            dpre[...], nv[:, cols], TN, preferred_element_type=F32
        ).astype(BF16)
        there = pl.multiple_of((2 * b + yhi) * run, run)
        gfp[b, units:] = lax.dot_general(
            act[...], dresid(there, run), TN, preferred_element_type=F32
        ).astype(BF16)

    last = ring_scatter(send, z, nz, gfp, rings[2 * h : 3 * h], rings[3 * h :], make_gf)
    step(last)
    finish(ring)
    ghs[...] = ring_result(z, ghp, rings[:h], rings[h : 2 * h]).astype(BF16)
    halves = [pl.ds(pl.multiple_of(i * run, run), run) for i in (yhi, 1 - yhi)]
    crossed = send.go(ghs.at[:, halves[1]], ghx, ("col", 0, 1))
    step(last)
    step(last)
    step(last)
    crossed.wait_recv()
    for k in range(nz):
        src = slice(k * tw, (k + 1) * tw)
        for value, half in ((ghs[src, halves[0]], yhi), (ghx[src, :], 1 - yhi)):
            ghv[pl.ds(pl.multiple_of(k * 2 * tw + half * tw, tw), tw), :] = value.astype(F32)
    gh_out[...] = ghv[...].T
    finish(last)
    result = ring_result(z, gfp, rings[2 * h : 3 * h], rings[3 * h :])
    gi_out[...] = result[:units]
    go_out[...] = result[units:]
    send.drain()


VM = pl.BlockSpec(memory_space=pltpu.VMEM)
ANY = pl.BlockSpec(memory_space=pl.ANY)
SD = jax.ShapeDtypeStruct


def params(cid):
    return pltpu.CompilerParams(
        collective_id=cid, has_side_effects=True, vmem_limit_bytes=56 * 1024 * 1024
    )


def sems(remote, local):
    dma = pltpu.SemaphoreType.DMA
    return [dma((remote,)), dma((remote,)), dma((local,))]


def call_forward(feats, gain_in, w_in, w_out, gain, hw, buf, pos, toks):
    tok, width = feats.shape
    units = w_in.shape[0]
    _, rows, cols = hw.shape
    nz = lax.axis_size("z")
    tw = buf.shape[0]
    scratch = [
        pltpu.VMEM((tok, width), BF16),
        pltpu.VMEM(w_in.shape, BF16),
        pltpu.VMEM((units, width), BF16),
        pltpu.VMEM(buf.shape, BF16),
        pltpu.VMEM(buf.shape[::-1], BF16),
        pltpu.VMEM((tok, width), BF16),
        pltpu.VMEM(CUBE[1:] + (BLK, width), BF16),
        pltpu.VMEM((tok, units), F32),
        pltpu.VMEM(CUBE[1:] + (BLK, width), BF16),
        pltpu.VMEM(CUBE[2:] + (BLK, width), BF16),
        pltpu.VMEM(CUBE + (BLK, width), BF16),
        pltpu.VMEM((nz, 2, rows, cols), BF16),
        pltpu.VMEM((nz, tok, 2 * tw), BF16),
        pltpu.VMEM((nz, tok, 2 * tw), BF16),
    ]
    return pl.pallas_call(
        forward_kernel,
        out_shape=(
            SD(CUBE + (BLK, width), BF16),
            SD((nz, 2, rows, cols), BF16),
            SD((BLK, width), F32),
            SD((BLK, 128), F32),
            SD((2, tok, width // 2), BF16),
            SD((2, tok, units), F32),
            SD((nz, tok, 2 * tw), BF16),
            SD((2,) + toks.shape, jnp.int32),
        ),
        in_specs=[ANY, VM, ANY, ANY, VM, ANY, ANY, VM, ANY],
        out_specs=(ANY, ANY, VM, VM, ANY, VM, ANY, ANY),
        scratch_shapes=scratch + sems(96, 48) + landing(ICI3, width),
        compiler_params=params(1),
        cost_estimate=pl.CostEstimate(flops=10**10, bytes_accessed=10**8, transcendentals=0),
        name="forward_plane",
    )(feats, gain_in[None], w_in, w_out, gain[None], hw, buf, pos, toks)


def call_backward(first_col, final, head, target, w_out, normed, pre, toks, resid, scale, gain, run):
    n_tok, width = final.shape
    n_col = head.shape[1]
    units = w_out.shape[0]
    nz = lax.axis_size("z")
    vm = pltpu.VMEM
    scratch = [
        vm((n_tok, width), BF16),
        vm((width, n_col), BF16),
        vm(target.shape, BF16),
        vm(w_out.shape, BF16),
        vm(normed.shape, BF16),
        vm((n_tok, n_col), F32),
        vm((n_tok, n_col), F32),
        vm((8, n_tok), F32),
        vm((7, 8, n_tok), F32),
        vm((8, n_tok), F32),
        vm((3, 8, n_tok), F32),
        vm((128, n_tok), F32),
        vm((n_tok, n_col), BF16),
        vm(CUBE + (BLK, width), BF16),
        vm((2,) * 4 + (BLK, width), BF16),
        vm(CUBE + (BLK, width), BF16),
        vm((nz, n_col, 2 * run), BF16),
        vm((n_col, 2 * run), BF16),
        vm((n_col, run), BF16),
        vm((2 * n_col, run), F32),
        vm((nz, 2 * units, run), BF16),
        vm((n_tok, units), F32),
        vm((n_tok, units), BF16),
        vm((n_tok, units), BF16),
    ]
    rings = [vm((n_col, 2 * run), BF16) for _ in range(nz)]
    rings += [vm((2 * units, run), BF16) for _ in range(nz)]
    return pl.pallas_call(
        functools.partial(backward_kernel, run, first_col),
        out_shape=(SD((run, 2 * n_col), F32), SD((units, run), F32), SD((units, run), F32)),
        in_specs=[ANY] * 5 + [VM] * 5,
        out_specs=(VM, VM, VM),
        scratch_shapes=scratch + sems(120, 8) + rings + landing(ICI4, width),
        compiler_params=params(3),
        cost_estimate=pl.CostEstimate(flops=10**10, bytes_accessed=10**8, transcendentals=0),
        name="backward_plane",
    )(final, head, target, w_out, normed, pre, toks, resid, scale, gain[None])


def body(
    features, token_ids, positions, target_buffer, norm_gain, final_gain, w_in, w_out, head_weight
):
    nz = lax.axis_size("z")
    rows, cols = head_weight.shape
    tok, width = features.shape
    units = w_in.shape[1]
    tw = target_buffer.shape[1]

    hw = head_weight.reshape(rows, nz, 2, tw).transpose(2, 0, 1, 3).reshape(2, rows, cols // 2)
    pos = jnp.zeros((128, tok), F32).at[: 2 * nz].set(positions.reshape(2 * nz, tok).astype(F32))
    toks = jnp.zeros((8, 128), jnp.int32).at[: tok // 128].set(token_ids.reshape(tok // 128, 128))
    final, head, resid, scale, normed, pre, target, toks = call_forward(
        features, norm_gain, w_in.T, w_out, final_gain, hw, target_buffer.T, pos, toks
    )
    tokens = jnp.zeros((8, 2 * tok), F32).at[0].set(
        toks[:, : tok // 128].reshape(2 * tok).astype(F32)
    )

    def first_col():
        block = (lax.axis_index("ylo") * 4 + lax.axis_index("x")) * 2 + lax.axis_index("core")
        return block * cols + lax.axis_index("yhi") * tw

    gh, gi, go = call_backward(
        first_col,
        final.reshape(2 * tok, width),
        head.reshape(width, cols // 2),
        target,
        w_out,
        normed.reshape(2 * tok, width // 2),
        pre.reshape(2 * tok, units),
        tokens,
        resid,
        scale,
        final_gain,
        rows,
    )
    return (gh, gi.T, go)


def solution(mesh):
    names = ("ylo", "x", "core", "z", "yhi")
    fine = Mesh(mesh.devices.reshape(2, 4, 2, -1, 2), names)
    v = ("ylo", "x", "core")
    d = ("z", "yhi")
    return jax.shard_map(
        body,
        mesh=fine,
        in_specs=(
            P(d, None),
            P(d),
            P(),
            P(None, v + d),
            P(),
            P(),
            P(None, v),
            P(v, None),
            P(d, v),
        ),
        out_specs=(P(d, v), P(d, v), P(v, d)),
        check_vma=False,
    )
```

```python
import functools
import jax
import jax.numpy as jnp
from jax import lax
from jax.experimental import pallas as pl
from jax.experimental.pallas import tpu as pltpu
from jax.sharding import Mesh, PartitionSpec as P

EPS = 1e-05
HARD = 0.5
MESH = pl.DeviceIdType.MESH
LEAD = ("YB", "core", "XA", "YA", "XB")
REST = ("YB", "XA", "YA", "XB")
ICI3 = ("XA", "YA", "XB")
ICI4 = ("XA", "YA", "XB", "YB")
CUBE = (2,) * 5
BLK = 16
F32 = jnp.float32
BF16 = jnp.bfloat16


FORWARD_STEPS = ((1, 0, 2, 0, 1), (1, 0, 1, 1))
BACKWARD_STEPS = ((0, 0, 1, 1, 0, 1), (0, 1, 1, 1))


def place():
    x, ylo, yhi, core, z = (lax.axis_index(n) for n in ("x", "ylo", "yhi", "core", "z"))
    nz = lax.axis_size("z")
    y = 2 * yhi + ylo
    odd = lax.rem(x, 2)
    bits = {
        "core": core,
        "XA": lax.rem(lax.div(x + 1, 2), 2),
        "XB": lax.div(x, 2),
        "YA": lax.rem(lax.div(y + 1, 2), 2),
        "YB": yhi,
    }
    to = {
        "core": {"core": 1 - core},
        "XA": {"x": x + 1 - 2 * odd},
        "XB": {"x": lax.rem(x + 3 + 2 * odd, 4)},
        "YA": {"ylo": 1 - ylo},
        "YB": {"ylo": 1 - ylo, "yhi": 1 - yhi},
        "pair": {"yhi": 1 - yhi},
        "up": {"z": lax.rem(z + 1, nz)},
        "down": {"z": lax.rem(z + nz - 1, nz)},
    }
    for i in range(1, nz):
        to[i] = {"z": lax.rem(z + i, nz)}
    for i in range(4):
        for c in range(2):
            to["row", i, c] = {"x": lax.rem(x + i, 4), "core": lax.rem(core + c, 2)}
    for a in range(2):
        for b in range(2):
            to["col", a, b] = {"ylo": lax.rem(ylo + a, 2), "yhi": lax.rem(yhi + b, 2)}
    return bits, to, z, nz


def at(names, fixed, cols=None):
    where = tuple(fixed.get(n, slice(None)) for n in names)
    return where + (slice(None), slice(None) if cols is None else pl.ds(*cols))


def corners(names):
    out = [{}]
    for n in names:
        out = [dict(o, **{n: v}) for o in out for v in (0, 1)]
    return out


class Sender:
    def __init__(self, send_sem, recv_sem, to):
        self.send_sem, self.recv_sem, self.to = send_sem, recv_sem, to
        self.n = 0
        self.open = []

    def go(self, src, dst, dim):
        n = self.n
        c = pltpu.make_async_remote_copy(
            src_ref=src,
            dst_ref=dst,
            send_sem=self.send_sem.at[n],
            recv_sem=self.recv_sem.at[n],
            device_id=self.to[dim],
            device_id_type=MESH,
        )
        c.start()
        self.n += 1
        self.open.append(c)
        return c

    def drain(self):
        for c in self.open:
            c.wait_send()
        self.open = []


class Local:
    def __init__(self, sem):
        self.sem = sem
        self.n = 0

    def go(self, src, dst):
        c = pltpu.make_async_copy(src, dst, self.sem.at[self.n])
        c.start()
        self.n += 1
        return c


def colours(n, width):
    tiles = width // 128
    edges = [128 * (tiles * k // n) for k in range(n + 1)]
    return [(edges[k], edges[k + 1] - edges[k]) for k in range(n)]


def greet(to, dims):
    barrier = pltpu.get_barrier_semaphore()
    for d in dims:
        pl.semaphore_signal(barrier, inc=1, device_id=to[d], device_id_type=MESH)
    return lambda: pl.semaphore_wait(barrier, len(dims))


def meet(to, dims):
    greet(to, dims)()


def step(thread):
    return next(thread, None)


def finish(thread):
    for _ in thread:
        pass


def region(names, order, bits, j, core):
    fixed = {m: bits[m] for m in order[:j]}
    if j < len(order):
        fixed[order[j]] = 1 - bits[order[j]]
    if core:
        fixed["core"] = bits["core"]
    return fixed, [m for m in names if m not in fixed]


def reduce_cube(send, bits, names, dims, width, part, total, landed):
    rest = tuple(n for n in names if n != "core")
    n = len(dims)
    cuts = colours(n, width)
    orders = [[dims[(k + i) % n] for i in range(n)] for k in range(n)]
    first, second = [], []
    for keep, held in ((1, first), (0, second)):
        for k in range(n):
            d = dims[k]
            bit = 1 - bits[d] if keep else bits[d]
            src = part.at[at(names, {"core": 1 - bits["core"], d: bit}, cuts[k])]
            dst = total.at[at(rest, {d: bit}, cuts[k])]
            held.append(send.go(src, dst, "core"))

    def merge(k, bit):
        d = dims[k]
        for f in corners([m for m in rest if m != d]):
            f = dict(f, **{d: bit})
            w = at(rest, f, cuts[k])
            total[w] = total[w] + part[at(names, dict(f, core=bits["core"]), cuts[k])]

    slots = iter(landed)
    coming = {}

    def start(k, i):
        o = orders[k]
        for j in range(i + 1, n + 1):
            fixed = region(rest, o, bits, j, False)[0]
            fixed[o[i]] = 1 - bits[o[i]]
            slot = next(slots)
            src = total.at[at(rest, fixed, cuts[k])]
            coming[k, i, j] = (send.go(src, slot, o[i]), slot)

    yield
    for k in range(n):
        first[k].wait_recv()
        merge(k, 1 - bits[dims[k]])
        start(k, 0)
    yield
    for k in range(n):
        second[k].wait_recv()
        merge(k, bits[dims[k]])
    for j in range(1, n + 1):
        yield
        for k in range(n):
            fixed, free = region(rest, orders[k], bits, j, False)
            got = [coming[k, i, j] for i in range(j)]
            for c, _ in got:
                c.wait_recv()
            for f in corners(free):
                w = at(rest, dict(f, **fixed), cuts[k])
                value = total[w]
                for _, slot in got:
                    value = value + slot[tuple(f[m] for m in free)]
                total[w] = value
            if j < n:
                start(k, j)


def landing(dims, width):
    n = len(dims)
    cuts = colours(n, width)

    def room(k, i):
        return [
            pltpu.VMEM((2,) * (n - 1 - j) + (BLK, cuts[k][1]), BF16) for j in range(i + 1, n + 1)
        ]

    return [slot for i in range(n) for k in range(n) for slot in room(k, i)]


def gather_cube(send, bits, dims, width, full, names=LEAD):
    n = len(dims)
    cuts = colours(n, width)
    orders = [[dims[(k + i) % n] for i in range(n)] for k in range(n)]
    own = full.at[at(names, bits)]
    direct = {d: send.go(own, own, d) for d in dims}
    arriving = [send.go(own, own, "core")]
    coming = {(k, j): [] for k in range(n) for j in range(n)}
    for i in range(n):
        yield
        for k in range(n):
            o = orders[k]
            if i == 0:
                direct[o[0]].wait_recv()
            for c in coming[k, i]:
                c.wait_recv()
            fixed = {m: bits[m] for m in names if m not in o[:i]}
            fixed[o[i]] = 1 - bits[o[i]]
            piece = full.at[at(names, fixed, cuts[k])]
            for j in range(i + 1, n):
                coming[k, j].append(send.go(piece, piece, o[j]))
            arriving.append(send.go(piece, piece, "core"))
    for c in arriving:
        c.wait_recv()


def ring_gather(send, z, nz, full, own, other, late):
    half = nz // 2
    rows = (own, other)

    def block(i, q):
        return full.at[lax.rem(z + nz + i, nz), rows[q]]

    flying = {}

    def hop(s, q):
        for way, sign, short in (("up", -1, 0), ("down", 1, 1)):
            if s and (s < half or q == short):
                flying[way, q].wait_recv()
            if s + 1 < half or (s + 1 == half and q == short):
                flying[way, q] = send.go(block(sign * s, q), block(sign * s, q), way)

    hop(0, 0)
    yield None
    hop(1, 0)
    yield None
    late.wait_recv()
    hop(0, 1)
    yield 0
    for s in range(1, half + 1):
        if s + 1 <= half:
            hop(s + 1, 0)
            yield None
        hop(s, 1)
        yield s


def ring_scatter(send, z, nz, part, ups, downs, cut, prepare):
    half = nz // 2
    made = set()

    def mine(i, q):
        b = lax.rem(z + nz + i, nz)
        if (i % nz, q) not in made:
            made.add((i % nz, q))
            prepare(b, q)
        return part.at[(b,) + cut[q]]

    flying = {}
    ways = (("up", ups, 1), ("down", downs, -1))
    for q in (1, 0):
        for way, landed, sign in ways:
            s = 0 if q == (0 if way == "up" else 1) else 1
            if s < half:
                flying[way, s, q] = send.go(mine(sign * (half - s), q), landed[s].at[cut[q]], way)
        yield
    for s in range(half):
        for lead in (1, 0) if s else (0,):
            for way, landed, sign in ways:
                q = lead if way == "up" else 1 - lead
                own = mine(sign * (half - 1 - s), q)
                flying[way, s, q].wait_recv()
                if s + 1 < half:
                    ref = landed[s].at[cut[q]]
                    ref[...] = ref[...] + own[...]
                    flying[way, s + 1, q] = send.go(ref, landed[s + 1].at[cut[q]], way)
            yield
    for q in range(2):
        mine(0, q)


def ring_result(z, part, ups, downs, cut, q):
    total = part[(z,) + cut[q]].astype(F32)
    sides = (ups, downs) if len(ups) > 1 else ((ups, downs)[q],)
    for side in sides:
        total = total + side[-1][cut[q]].astype(F32)
    return total


def runs_of(value, parity, tw):
    out = []
    for k in range(value.shape[1] // (4 * tw)):
        starts = [(2 * (2 * k + i) + parity) * tw for i in range(2)]
        out.append(jnp.concatenate([value[:, s : s + tw] for s in starts], 1))
    return jnp.concatenate(out, 1)


def own_row(bits):
    r = bits["core"]
    for n in ("XA", "YA", "XB"):
        r = 2 * r + bits[n]
    return r * BLK


def exchange_stats(send, own, near, held, far, out):
    def merge(src, slots, peers, dst):
        flying = [send.go(src, slots.at[i], p) for i, p in enumerate(peers)]
        for c in flying:
            c.wait_recv()
        parts = [src[...]] + [slots[i] for i in range(len(peers))]
        tops = [p[0:2] for p in parts]
        top = functools.reduce(jnp.maximum, tops)
        total = functools.reduce(
            jnp.add, [p[2:4] * jnp.exp(t - top) for p, t in zip(parts, tops)]
        )
        dst[0:2] = top
        dst[2:4] = total

    held[4:8] = jnp.zeros((4, held.shape[1]), F32)
    merge(own, near, [("row", i, c) for i in range(4) for c in range(2) if i or c], held)
    merge(held, far, [("col", a, b) for a in range(2) for b in range(2) if a or b], out)


NT = (((1,), (1,)), ((), ()))
TN = (((0,), (0,)), ((), ()))


def kernel(
    run, first_col,
    feats, gain_in, w_in, w_out, gain, hw, buf, pos, toks,
    gh_out, gf_out,
    fv, hs, pp, tk, tk2, w1, w2, bv, bn, normed, other, pre, part, total, full, head, ordered, target,
    pexp, lg, own, near, held, far, back, dl, dres, ghp, ghx, gfp, act, dpre,
    send_sem, recv_sem, local_sem, *landed,
):
    bits, to, z, nz = place()
    yhi = bits["YB"]
    tok, width = fv.shape
    n_tok = 2 * tok
    n_col = head.shape[2]
    units = w1.shape[0]
    tw = bv.shape[0]
    half = nz // 2
    names = LEAD[1:]
    gh_rings, landed = landed[:nz], landed[nz:]
    n_forward = len(landing(ICI3, width))
    peers = [("row", i, c) for i in range(4) for c in range(2) if i or c]
    peers += [("col", a, b) for a in range(2) for b in range(2) if a or b]
    greeted = greet(to, peers + ["up", "down"] + list(range(2, nz - 1)))
    local = Local(local_sem)
    got_f = local.go(feats, fv)
    got_w1 = local.go(w_in, w1)
    got_w2 = local.go(w_out, w2)
    got_b = local.go(buf, bv)

    here = pl.ds(pl.multiple_of(yhi * run, run), run)
    there = pl.ds(pl.multiple_of((1 - yhi) * run, run), run)
    both = hw[...].astype(F32)
    both = [runs_of(both, p, tw) for p in range(2)]
    head[z, here] = jnp.where(yhi == 0, both[0], both[1]).astype(BF16)
    hs[...] = jnp.where(yhi == 0, both[1], both[0]).astype(BF16)
    tk[...] = jnp.zeros(tk.shape, jnp.int32)
    tk[0 : toks.shape[0]] = toks[...]
    pp[...] = jnp.zeros(pp.shape, F32)
    pp[0 : pos.shape[0]] = pos[...].astype(F32)

    got_f.wait()
    chunk = 64

    def norm_rows(i, _):
        rows = pl.ds(pl.multiple_of(i * chunk, chunk), chunk)
        x = fv[rows, :].astype(F32)
        r = lax.rsqrt(jnp.mean(x * x, -1, keepdims=True) + EPS)
        normed[rows, :] = (x * r * gain_in[...]).astype(BF16)
        return 0

    lax.fori_loop(0, tok // chunk, norm_rows, 0)
    greeted()
    send = Sender(send_sem, recv_sem, to)
    late = send.go(hs, head.at[z, here], "pair")
    ring = ring_gather(send, z, nz, head, here, there, late)
    step(ring)
    swapped = [send.go(tk, tk2, "pair")]
    mine = pl.ds(pl.multiple_of(own_row(bits), BLK), BLK)
    crossed = send.go(normed.at[mine], other.at[at(names, bits)], "YB")

    deep = width // 4

    def project(slot, rows):
        for c in range(4):
            k = pl.ds(c * deep, deep)
            prod = lax.dot_general(rows(k), w1[:, k], NT, preferred_element_type=F32)
            pre[slot] = prod if c == 0 else pre[slot] + prod

    got_w1.wait()
    project(0, lambda k: normed[:, k])
    v = pre[0]
    forward_act = (v * jax.nn.sigmoid(v)).astype(BF16)
    got_w2.wait()
    wide = width // 8
    first_part, first_total = part.at[0], total.at[0]
    for c in range(8):
        cols = (c * wide, wide)
        block = jnp.dot(forward_act, w2[:, pl.ds(*cols)], preferred_element_type=F32).astype(BF16)
        for i, f in enumerate(corners(names)):
            first_part[at(names, f, cols)] = block[i * BLK : (i + 1) * BLK]

    got_b.wait()
    n_buf = bv.shape[1]
    piece = 1024 if n_buf % 1024 == 0 else n_buf
    pos_t = pp[...].T

    def ordered_rows(i):
        dest = lax.rem(z + i, nz)
        lane = lax.broadcasted_iota(jnp.int32, pos_t.shape, 1)
        each = tok // 128
        there = [
            jnp.concatenate(
                [
                    jnp.sum(
                        jnp.where(lane == (2 * dest + h) * each + e, pos_t, 0.0), 1, keepdims=True
                    )
                    for e in range(each)
                ],
                0,
            )
            for h in range(2)
        ]
        cols = lax.broadcasted_iota(jnp.int32, (tok, piece), 1).astype(F32)

        def inner(t, sums):
            rows = bn[pl.ds(pl.multiple_of(t * piece, piece), piece), :]
            out = []
            for h in range(2):
                hot = jnp.where(there[h] - (t * piece).astype(F32) == cols, 1.0, 0.0).astype(BF16)
                out.append(sums[h] + jnp.dot(hot, rows, preferred_element_type=F32))
            return tuple(out)

        zero = jnp.zeros((tok, bv.shape[0]), F32)
        a, b = lax.fori_loop(0, n_buf // piece, inner, (zero, zero))
        return jnp.concatenate([a, b], 1).astype(BF16)

    def gather_target():
        for i in range(1, nz):
            ordered[i] = ordered_rows(i)
            way = "up" if i == 1 else "down" if i == nz - 1 else i
            swapped.append(send.go(ordered.at[i], target.at[z], way))
            yield
        target[z] = ordered_rows(0)
        yield

    def gather_other():
        crossed.wait_recv()
        yield from gather_cube(send, bits, ICI3, width, other, names)

    side = gather_target()
    cross = gather_other()
    ready = []

    def advance(count):
        for _ in range(count):
            s = step(ring)
            if s is not None:
                ready.extend([s] if s in (0, half) else [s, -s])

    reduce = reduce_cube(send, bits, names, ICI3, width, first_part, first_total, landed[:n_forward])
    for i, _ in enumerate(reduce):
        if i == 0:
            bn[...] = bv[...].T
        step(side)
        advance(FORWARD_STEPS[0][i])
        if i >= 1:
            step(cross)
    hidden = first_total[at(ICI3, bits)].astype(F32)
    resid = fv[mine, :].astype(F32) + hidden
    rscale = lax.rsqrt(jnp.mean(resid * resid, -1, keepdims=True) + EPS)
    full[at(LEAD, bits)] = (resid * rscale * gain[...]).astype(BF16)
    for i, _ in enumerate(gather_cube(send, bits, ICI4, width, full)):
        step(side)
        advance(FORWARD_STEPS[1][i])
    finish(side)
    finish(cross)
    project(1, lambda k: other[at(names, {}, (k.start, k.size))].reshape(tok, k.size))

    started = []

    def add_logits():
        while ready:
            b = lax.rem(z + nz + ready.pop(0), nz)
            cols = (pl.multiple_of(b * 2 * run, 2 * run), 2 * run)
            rows = full[at(LEAD, {}, cols)].reshape(n_tok, 2 * run)
            prod = jnp.dot(rows, head[b], preferred_element_type=F32)
            lg[...] = lg[...] + prod if started else prod
            started.append(b)

    add_logits()
    for c in swapped:
        c.wait_recv()
    for k in range(nz // 2):
        for s in range(2):
            lanes = slice(s * tw, (s + 1) * tw)
            two = [target[2 * k + i].astype(F32)[:, lanes] for i in range(2)]
            pexp[s * tok : (s + 1) * tok, k * 2 * tw : (k + 1) * 2 * tw] = jnp.concatenate(two, 1)
    t = pexp[...]
    top_p = jnp.max(t, -1, keepdims=True)
    t = jnp.exp(t - top_p)
    pexp[...] = t
    sum_p = jnp.sum(t, -1, keepdims=True)
    for s in ring:
        if s is not None:
            ready.extend([s] if s in (0, half) else [s, -s])
            add_logits()
    t = lg[...]
    top_q = jnp.max(t, -1, keepdims=True)
    t = jnp.exp(t - top_q)
    lg[...] = t
    sum_q = jnp.sum(t, -1, keepdims=True)
    lane = lax.broadcasted_iota(jnp.int32, (n_tok, 128), 1)
    columns = jnp.where(
        lane == 0, top_q, jnp.where(lane == 1, top_p, jnp.where(lane == 2, sum_q, sum_p))
    )
    own[...] = columns.T[0:8]
    back[...] = jnp.zeros(back.shape, F32)
    for i in range(n_tok // 128):
        e = i % (tok // 128)
        line = jnp.where(yhi == i // (tok // 128), tk[e : e + 1], tk2[e : e + 1])
        back[8:9, i * 128 : (i + 1) * 128] = line.astype(F32)
    send.drain()
    exchange_stats(send, own, near, held, far, back)
    columns = back[...].T
    all_q, all_p, tot_q, tot_p, token = (columns[:, i : i + 1] for i in (0, 1, 2, 3, 8))
    q = lg[...] * (jnp.exp(top_q - all_q) / tot_q)
    p = pexp[...] * (jnp.exp(top_p - all_p) / tot_p)
    lane = lax.broadcasted_iota(jnp.int32, (n_tok, n_col), 1)
    shift = tw.bit_length() - 1
    column = first_col() + lane + jnp.left_shift(jnp.right_shift(lane, shift), shift)
    onehot = jnp.where(token.astype(jnp.int32) == column, 1.0, 0.0)
    dl[...] = (q - p + HARD * (q - onehot)).astype(BF16)

    split = n_col // 2
    rows_cut = [(pl.ds(i * split, split), slice(None)) for i in range(2)]

    def make_gh(b, q):
        cols = (pl.multiple_of(b * 2 * run, 2 * run), 2 * run)
        rows = full[at(LEAD, {}, cols)].reshape(n_tok, 2 * run)
        ghp[(b,) + rows_cut[q]] = lax.dot_general(
            dl[:, q * split : (q + 1) * split], rows, TN, preferred_element_type=F32
        ).astype(BF16)

    gh_ups, gh_downs = gh_rings[:half], gh_rings[half:]
    ring = ring_scatter(send, z, nz, ghp, gh_ups, gh_downs, rows_cut, make_gh)
    step(ring)
    step(ring)
    block_rows = head.shape[1]
    for c in range(nz):
        cols = (c * block_rows, block_rows)
        block = lax.dot_general(dl[...], head[c], NT, preferred_element_type=F32).astype(BF16)
        for i, f in enumerate(corners(LEAD)):
            part[at(LEAD, f, cols)] = block[i * BLK : (i + 1) * BLK]
    reduce = reduce_cube(send, bits, LEAD, ICI4, width, part, total, landed[n_forward:])
    for i, _ in enumerate(reduce):
        for _ in range(BACKWARD_STEPS[0][i]):
            step(ring)
    dfinal = total[at(REST, bits)].astype(F32)
    scaled = dfinal * gain[...]
    inner = jnp.sum(scaled * resid, -1, keepdims=True)
    dres[at(LEAD, bits)] = (
        rscale * scaled - resid * (rscale * rscale * rscale / width * inner)
    ).astype(BF16)
    for i, _ in enumerate(gather_cube(send, bits, ICI4, width, dres)):
        for _ in range(BACKWARD_STEPS[1][i]):
            step(ring)
    finish(ring)

    def dresid(start, size):
        return dres[at(LEAD, {}, (start, size))].reshape(n_tok, size)

    def by_half(a, b):
        return jnp.where(yhi == 0, a, b), jnp.where(yhi == 0, b, a)

    v = jnp.concatenate(by_half(pre[0], pre[1]), 0)
    sig = jax.nn.sigmoid(v)
    act[...] = (v * sig).astype(BF16)
    lanes_cut = [(slice(None), pl.ds(i * run, run)) for i in range(2)]

    def make_gf(b, q):
        start = pl.multiple_of((2 * b + yhi) * run, run)
        if q:
            left, right = act[...], dresid(start, run)
        else:
            rows = other[at(names, {}, (start, run))].reshape(tok, run)
            left = dpre[...]
            right = jnp.concatenate(by_half(normed[:, pl.ds(start, run)], rows), 0)
        gfp[(b,) + lanes_cut[q]] = lax.dot_general(
            left, right, TN, preferred_element_type=F32
        ).astype(BF16)

    gf_ups = [head.at[i, 0:units] for i in range(half)]
    gf_downs = [head.at[half + i, 0:units] for i in range(half)]
    last = ring_scatter(send, z, nz, gfp, gf_ups, gf_downs, lanes_cut, make_gf)
    step(last)
    for c in range(4):
        k = pl.ds(c * deep, deep)
        prod = lax.dot_general(dresid(c * deep, deep), w2[:, k], NT, preferred_element_type=F32)
        lg[:, 0:units] = prod if c == 0 else lg[:, 0:units] + prod
    dpre[...] = (lg[:, 0:units] * sig * (1.0 + v * (1.0 - sig))).astype(BF16)
    step(last)

    for i in range(2):
        dl[rows_cut[i]] = ring_result(z, ghp, gh_ups, gh_downs, rows_cut, i).astype(BF16)
    crossed = send.go(dl.at[:, there], ghx, ("col", 0, 1))
    for _ in range(3):
        step(last)
    crossed.wait_recv()
    for k in range(nz):
        src = slice(k * tw, (k + 1) * tw)
        for value, side in ((dl[src, here], yhi), (ghx[src, :], 1 - yhi)):
            gh_out[pl.ds(pl.multiple_of(k * 2 * tw + side * tw, tw), tw), :] = value
    finish(last)
    for i in range(2):
        gf_out[lanes_cut[i]] = ring_result(z, gfp, gf_ups, gf_downs, lanes_cut, i).astype(BF16)
    send.drain()


VM = pl.BlockSpec(memory_space=pltpu.VMEM)
ANY = pl.BlockSpec(memory_space=pl.ANY)
SD = jax.ShapeDtypeStruct


def params(cid):
    return pltpu.CompilerParams(
        collective_id=cid, has_side_effects=True, vmem_limit_bytes=62 * 1024 * 1024
    )


def sems(remote, local):
    dma = pltpu.SemaphoreType.DMA
    return [dma((remote,)), dma((remote,)), dma((local,))]


def call_step(first_col, feats, gain_in, w_in, w_out, gain, hw, buf, pos, toks):
    tok, width = feats.shape
    units = w_in.shape[0]
    run, n_col = hw.shape[0], hw.shape[1] // 2
    nz = lax.axis_size("z")
    tw = buf.shape[0]
    n_tok = 2 * tok
    vm = pltpu.VMEM
    scratch = [
        vm((tok, width), BF16),
        vm((run, n_col), BF16),
        vm((128, 128), F32),
        vm((8, 128), jnp.int32),
        vm((8, 128), jnp.int32),
        vm(w_in.shape, BF16),
        vm(w_out.shape, BF16),
        vm(buf.shape, BF16),
        vm(buf.shape[::-1], BF16),
        vm((tok, width), BF16),
        vm(CUBE[1:] + (BLK, width), BF16),
        vm((2, tok, units), F32),
        vm(CUBE + (BLK, width), BF16),
        vm(CUBE[1:] + (BLK, width), BF16),
        vm(CUBE + (BLK, width), BF16),
        vm((nz, 2 * run, n_col), BF16),
        vm((nz, tok, 2 * tw), BF16),
        vm((nz, tok, 2 * tw), BF16),
        vm((n_tok, n_col), F32),
        vm((n_tok, n_col), F32),
        vm((8, n_tok), F32),
        vm((7, 8, n_tok), F32),
        vm((8, n_tok), F32),
        vm((3, 8, n_tok), F32),
        vm((128, n_tok), F32),
        vm((n_tok, n_col), BF16),
        vm(CUBE + (BLK, width), BF16),
        vm((nz, n_col, 2 * run), BF16),
        vm((n_col, run), BF16),
        vm((nz, units, 2 * run), BF16),
        vm((n_tok, units), BF16),
        vm((n_tok, units), BF16),
    ]
    rings = [vm((n_col, 2 * run), BF16) for _ in range(nz)]
    return pl.pallas_call(
        functools.partial(kernel, run, first_col),
        out_shape=(SD((2 * n_col, run), BF16), SD((units, 2 * run), BF16)),
        in_specs=[ANY, VM, ANY, ANY, VM, VM, ANY, VM, VM],
        out_specs=(VM, VM),
        scratch_shapes=scratch
        + sems(256, 4)
        + rings
        + landing(ICI3, width)
        + landing(ICI4, width),
        compiler_params=params(1),
        cost_estimate=pl.CostEstimate(flops=10**10, bytes_accessed=10**8, transcendentals=0),
        name="distill_step",
    )(feats, gain_in[None], w_in, w_out, gain[None], hw, buf, pos, toks)


def write_kernel(gh, gf, gh_out, gi_out, go_out):
    run = gi_out.shape[1]
    gh_out[...] = gh[...].astype(F32).T
    gi_out[...] = gf[:, 0:run].astype(F32)
    go_out[...] = gf[:, run:].astype(F32)


def call_write(gh, gf):
    run = gh.shape[1]
    half = SD((gf.shape[0], run), F32)
    return pl.pallas_call(
        write_kernel,
        out_shape=(SD((run, gh.shape[0]), F32), half, half),
        in_specs=[VM, VM],
        out_specs=(VM, VM, VM),
        compiler_params=pltpu.CompilerParams(vmem_limit_bytes=32 * 1024 * 1024),
        name="write_out",
    )(gh, gf)


def body(
    features, token_ids, positions, target_buffer, norm_gain, final_gain, w_in, w_out, head_weight
):
    cols = head_weight.shape[1]
    tw = target_buffer.shape[1]

    def first_col():
        block = (lax.axis_index("ylo") * 4 + lax.axis_index("x")) * 2 + lax.axis_index("core")
        return block * cols + lax.axis_index("yhi") * tw

    gh, gf = call_step(
        first_col,
        features,
        norm_gain,
        w_in.T,
        w_out,
        final_gain,
        head_weight,
        target_buffer.T,
        positions.reshape(-1, 128),
        token_ids.reshape(-1, 128),
    )
    gh, gi, go = call_write(gh, gf)
    return (gh, gi.T, go)


def solution(mesh):
    names = ("ylo", "x", "core", "z", "yhi")
    fine = Mesh(mesh.devices.reshape(2, 4, 2, -1, 2), names)
    v = ("ylo", "x", "core")
    d = ("z", "yhi")
    return jax.shard_map(
        body,
        mesh=fine,
        in_specs=(
            P(d, None),
            P(d),
            P(),
            P(None, v + d),
            P(),
            P(),
            P(None, v),
            P(v, None),
            P(d, v),
        ),
        out_specs=(P(d, v), P(d, v), P(v, d)),
        check_vma=False,
    )
```

```python
import functools
import jax
import jax.numpy as jnp
from jax import lax
from jax.experimental import pallas as pl
from jax.experimental.pallas import tpu as pltpu
from jax.sharding import Mesh, PartitionSpec as P

EPS = 1e-05
HARD = 0.5
MESH = pl.DeviceIdType.MESH
LEAD = ("YB", "core", "XA", "YA", "XB")
REST = ("YB", "XA", "YA", "XB")
ICI3 = ("XA", "YA", "XB")
ICI4 = ("XA", "YA", "XB", "YB")
CUBE = (2,) * 5
BLK = 16
F32 = jnp.float32
BF16 = jnp.bfloat16


FORWARD_STEPS = ((1, 1, 1, 0, 1), (1, 1, 1, 1))
BACKWARD_STEPS = ((0, 1, 1, 0, 1, 0), (1, 1, 0, 1))


def place():
    x, ylo, yhi, core, z = (lax.axis_index(n) for n in ("x", "ylo", "yhi", "core", "z"))
    nz = lax.axis_size("z")
    y = 2 * yhi + ylo
    odd = lax.rem(x, 2)
    bits = {
        "core": core,
        "XA": lax.rem(lax.div(x + 1, 2), 2),
        "XB": lax.div(x, 2),
        "YA": lax.rem(lax.div(y + 1, 2), 2),
        "YB": yhi,
    }
    to = {
        "core": {"core": 1 - core},
        "XA": {"x": x + 1 - 2 * odd},
        "XB": {"x": lax.rem(x + 3 + 2 * odd, 4)},
        "YA": {"ylo": 1 - ylo},
        "YB": {"ylo": 1 - ylo, "yhi": 1 - yhi},
        "pair": {"yhi": 1 - yhi},
        "up": {"z": lax.rem(z + 1, nz)},
        "down": {"z": lax.rem(z + nz - 1, nz)},
    }
    for i in range(1, nz):
        to[i] = {"z": lax.rem(z + i, nz)}
    for i in range(4):
        for c in range(2):
            to["row", i, c] = {"x": lax.rem(x + i, 4), "core": lax.rem(core + c, 2)}
    for a in range(2):
        for b in range(2):
            to["col", a, b] = {"ylo": lax.rem(ylo + a, 2), "yhi": lax.rem(yhi + b, 2)}
    return bits, to, z, nz


def at(names, fixed, cols=None):
    where = tuple(fixed.get(n, slice(None)) for n in names)
    return where + (slice(None), slice(None) if cols is None else pl.ds(*cols))


def corners(names):
    out = [{}]
    for n in names:
        out = [dict(o, **{n: v}) for o in out for v in (0, 1)]
    return out


class Sender:
    def __init__(self, send_sem, recv_sem, to):
        self.send_sem, self.recv_sem, self.to = send_sem, recv_sem, to
        self.n = 0
        self.open = []

    def go(self, src, dst, dim):
        n = self.n
        c = pltpu.make_async_remote_copy(
            src_ref=src,
            dst_ref=dst,
            send_sem=self.send_sem.at[n],
            recv_sem=self.recv_sem.at[n],
            device_id=self.to[dim],
            device_id_type=MESH,
        )
        c.start()
        self.n += 1
        self.open.append(c)
        return c

    def drain(self):
        for c in self.open:
            c.wait_send()
        self.open = []


class Local:
    def __init__(self, sem):
        self.sem = sem
        self.n = 0

    def go(self, src, dst):
        c = pltpu.make_async_copy(src, dst, self.sem.at[self.n])
        c.start()
        self.n += 1
        return c


def colours(n, width):
    tiles = width // 128
    edges = [128 * (tiles * k // n) for k in range(n + 1)]
    return [(edges[k], edges[k + 1] - edges[k]) for k in range(n)]


def greet(to, dims):
    barrier = pltpu.get_barrier_semaphore()
    for d in dims:
        pl.semaphore_signal(barrier, inc=1, device_id=to[d], device_id_type=MESH)
    return lambda: pl.semaphore_wait(barrier, len(dims))


def meet(to, dims):
    greet(to, dims)()


def step(thread):
    return next(thread, None)


def finish(thread):
    for _ in thread:
        pass


def region(names, order, bits, j, core):
    fixed = {m: bits[m] for m in order[:j]}
    if j < len(order):
        fixed[order[j]] = 1 - bits[order[j]]
    if core:
        fixed["core"] = bits["core"]
    return fixed, [m for m in names if m not in fixed]


def reduce_cube(send, bits, names, dims, width, part, total, landed):
    rest = tuple(n for n in names if n != "core")
    n = len(dims)
    cuts = colours(n, width)
    orders = [[dims[(k + i) % n] for i in range(n)] for k in range(n)]
    first, second = [], []
    for keep, held in ((1, first), (0, second)):
        for k in range(n):
            d = dims[k]
            bit = 1 - bits[d] if keep else bits[d]
            src = part.at[at(names, {"core": 1 - bits["core"], d: bit}, cuts[k])]
            dst = total.at[at(rest, {d: bit}, cuts[k])]
            held.append(send.go(src, dst, "core"))

    def merge(k, bit):
        d = dims[k]
        for f in corners([m for m in rest if m != d]):
            f = dict(f, **{d: bit})
            w = at(rest, f, cuts[k])
            total[w] = total[w] + part[at(names, dict(f, core=bits["core"]), cuts[k])]

    slots = iter(landed)
    coming = {}

    def start(k, i):
        o = orders[k]
        for j in range(i + 1, n + 1):
            fixed = region(rest, o, bits, j, False)[0]
            fixed[o[i]] = 1 - bits[o[i]]
            slot = next(slots)
            src = total.at[at(rest, fixed, cuts[k])]
            coming[k, i, j] = (send.go(src, slot, o[i]), slot)

    yield
    for k in range(n):
        first[k].wait_recv()
        merge(k, 1 - bits[dims[k]])
        start(k, 0)
    yield
    for k in range(n):
        second[k].wait_recv()
        merge(k, bits[dims[k]])
    for j in range(1, n + 1):
        yield
        for k in range(n):
            fixed, free = region(rest, orders[k], bits, j, False)
            got = [coming[k, i, j] for i in range(j)]
            for c, _ in got:
                c.wait_recv()
            for f in corners(free):
                w = at(rest, dict(f, **fixed), cuts[k])
                value = total[w]
                for _, slot in got:
                    value = value + slot[tuple(f[m] for m in free)]
                total[w] = value
            if j < n:
                start(k, j)


def landing(dims, width):
    n = len(dims)
    cuts = colours(n, width)

    def room(k, i):
        return [
            pltpu.VMEM((2,) * (n - 1 - j) + (BLK, cuts[k][1]), BF16) for j in range(i + 1, n + 1)
        ]

    return [slot for i in range(n) for k in range(n) for slot in room(k, i)]


def gather_cube(send, bits, dims, width, full, names=LEAD):
    n = len(dims)
    cuts = colours(n, width)
    orders = [[dims[(k + i) % n] for i in range(n)] for k in range(n)]
    own = full.at[at(names, bits)]
    direct = {d: send.go(own, own, d) for d in dims}
    arriving = [send.go(own, own, "core")]
    coming = {(k, j): [] for k in range(n) for j in range(n)}
    for i in range(n):
        yield
        for k in range(n):
            o = orders[k]
            if i == 0:
                direct[o[0]].wait_recv()
            for c in coming[k, i]:
                c.wait_recv()
            fixed = {m: bits[m] for m in names if m not in o[:i]}
            fixed[o[i]] = 1 - bits[o[i]]
            piece = full.at[at(names, fixed, cuts[k])]
            for j in range(i + 1, n):
                coming[k, j].append(send.go(piece, piece, o[j]))
            arriving.append(send.go(piece, piece, "core"))
    for c in arriving:
        c.wait_recv()


def ring_gather(send, z, nz, full, own, other, late):
    half = nz // 2
    rows = (own, other)

    def block(i, q):
        return full.at[lax.rem(z + nz + i, nz), rows[q]]

    flying = {}

    def hop(s, q):
        for way, sign, short in (("up", -1, 0), ("down", 1, 1)):
            if s and (s < half or q == short):
                flying[way, q].wait_recv()
            if s + 1 < half or (s + 1 == half and q == short):
                flying[way, q] = send.go(block(sign * s, q), block(sign * s, q), way)

    hop(0, 0)
    yield None
    hop(1, 0)
    yield None
    late.wait_recv()
    hop(0, 1)
    yield 0
    for s in range(1, half + 1):
        if s + 1 <= half:
            hop(s + 1, 0)
            yield None
        hop(s, 1)
        yield s


def ring_scatter(send, z, nz, part, ups, downs, cut, prepare):
    half = nz // 2
    made = set()

    def mine(i, q):
        b = lax.rem(z + nz + i, nz)
        if (i % nz, q) not in made:
            made.add((i % nz, q))
            prepare(b, q)
        return part.at[(b,) + cut[q]]

    flying = {}
    ways = (("up", ups, 1), ("down", downs, -1))
    for q in (1, 0):
        for way, landed, sign in ways:
            s = 0 if q == (0 if way == "up" else 1) else 1
            if s < half:
                flying[way, s, q] = send.go(mine(sign * (half - s), q), landed[s].at[cut[q]], way)
        yield
    up = [(1, 1), (0, 0)] + [t for s in range(2, half) for t in ((s, 1), (s - 1, 0))] + [(half - 1, 0)]
    order = [t for t in dict.fromkeys(up) if t[0] < half]
    down = [(0, 1)] + [t for s in range(1, half) for t in ((s, 0), (s, 1))]
    for event in zip(order, down):
        for (way, landed, sign), (s, q) in zip(ways, event):
            own = mine(sign * (half - 1 - s), q)
            flying[way, s, q].wait_recv()
            if s + 1 < half:
                ref = landed[s].at[cut[q]]
                ref[...] = ref[...] + own[...]
                flying[way, s + 1, q] = send.go(ref, landed[s + 1].at[cut[q]], way)
        yield
    for q in range(2):
        mine(0, q)


def ring_result(z, part, ups, downs, cut, q):
    total = part[(z,) + cut[q]].astype(F32)
    sides = (ups, downs) if len(ups) > 1 else ((ups, downs)[q],)
    for side in sides:
        total = total + side[-1][cut[q]].astype(F32)
    return total


def runs_of(value, parity, tw):
    out = []
    for k in range(value.shape[1] // (4 * tw)):
        starts = [(2 * (2 * k + i) + parity) * tw for i in range(2)]
        out.append(jnp.concatenate([value[:, s : s + tw] for s in starts], 1))
    return jnp.concatenate(out, 1)


def own_row(bits):
    r = bits["core"]
    for n in ("XA", "YA", "XB"):
        r = 2 * r + bits[n]
    return r * BLK


def exchange_stats(send, own, near, held, far, out):
    def merge(src, slots, peers, dst):
        flying = [send.go(src, slots.at[i], p) for i, p in enumerate(peers)]
        for c in flying:
            c.wait_recv()
        parts = [src[...]] + [slots[i] for i in range(len(peers))]
        tops = [p[0:2] for p in parts]
        top = functools.reduce(jnp.maximum, tops)
        total = functools.reduce(
            jnp.add, [p[2:4] * jnp.exp(t - top) for p, t in zip(parts, tops)]
        )
        dst[0:2] = top
        dst[2:4] = total

    held[4:8] = jnp.zeros((4, held.shape[1]), F32)
    merge(own, near, [("row", i, c) for i in range(4) for c in range(2) if i or c], held)
    merge(held, far, [("col", a, b) for a in range(2) for b in range(2) if a or b], out)


NT = (((1,), (1,)), ((), ()))
TN = (((0,), (0,)), ((), ()))


def kernel(
    run, first_col,
    feats, gain_in, w_in, w_out, gain, hw, buf, pos, toks,
    gh_out, gf_out,
    fv, hs, pp, tk, tk2, w1, w2, bv, bn, normed, other, pre, part, total, full, head, ordered, target,
    pexp, lg, own, near, held, far, back, dl, dres, ghp, ghx, gfp, act, dpre,
    send_sem, recv_sem, local_sem, *landed,
):
    bits, to, z, nz = place()
    yhi = bits["YB"]
    tok, width = fv.shape
    n_tok = 2 * tok
    n_col = head.shape[2]
    units = w1.shape[0]
    tw = bv.shape[0]
    half = nz // 2
    names = LEAD[1:]
    gh_rings, landed = landed[:nz], landed[nz:]
    n_forward = len(landing(ICI3, width))
    peers = [("row", i, c) for i in range(4) for c in range(2) if i or c]
    peers += [("col", a, b) for a in range(2) for b in range(2) if a or b]
    greeted = greet(to, peers + ["up", "down"] + list(range(2, nz - 1)))
    local = Local(local_sem)
    got_f = local.go(feats, fv)
    got_w1 = local.go(w_in, w1)
    got_w2 = local.go(w_out, w2)
    got_b = local.go(buf, bv)

    here = pl.ds(pl.multiple_of(yhi * run, run), run)
    there = pl.ds(pl.multiple_of((1 - yhi) * run, run), run)
    both = hw[...].astype(F32)
    both = [runs_of(both, p, tw) for p in range(2)]
    head[z, here] = jnp.where(yhi == 0, both[0], both[1]).astype(BF16)
    hs[...] = jnp.where(yhi == 0, both[1], both[0]).astype(BF16)
    tk[...] = jnp.zeros(tk.shape, jnp.int32)
    tk[0 : toks.shape[0]] = toks[...]
    pp[...] = jnp.zeros(pp.shape, F32)
    pp[0 : pos.shape[0]] = pos[...].astype(F32)

    got_f.wait()
    chunk = 64

    def norm_rows(i, _):
        rows = pl.ds(pl.multiple_of(i * chunk, chunk), chunk)
        x = fv[rows, :].astype(F32)
        r = lax.rsqrt(jnp.mean(x * x, -1, keepdims=True) + EPS)
        normed[rows, :] = (x * r * gain_in[...]).astype(BF16)
        return 0

    lax.fori_loop(0, tok // chunk, norm_rows, 0)
    greeted()
    send = Sender(send_sem, recv_sem, to)
    late = send.go(hs, head.at[z, here], "pair")
    ring = ring_gather(send, z, nz, head, here, there, late)
    step(ring)
    swapped = [send.go(tk, tk2, "pair")]
    mine = pl.ds(pl.multiple_of(own_row(bits), BLK), BLK)
    crossed = send.go(normed.at[mine], other.at[at(names, bits)], "YB")

    deep = width // 4

    def project(slot, rows):
        for c in range(4):
            k = pl.ds(c * deep, deep)
            prod = lax.dot_general(rows(k), w1[:, k], NT, preferred_element_type=F32)
            pre[slot] = prod if c == 0 else pre[slot] + prod

    got_w1.wait()
    project(0, lambda k: normed[:, k])
    v = pre[0]
    forward_act = (v * jax.nn.sigmoid(v)).astype(BF16)
    got_w2.wait()
    wide = width // 8
    first_part, first_total = part.at[0], total.at[0]
    for c in range(8):
        cols = (c * wide, wide)
        block = jnp.dot(forward_act, w2[:, pl.ds(*cols)], preferred_element_type=F32).astype(BF16)
        for i, f in enumerate(corners(names)):
            first_part[at(names, f, cols)] = block[i * BLK : (i + 1) * BLK]

    got_b.wait()
    n_buf = bv.shape[1]
    piece = 1024 if n_buf % 1024 == 0 else n_buf
    pos_t = pp[...].T

    def ordered_rows(i):
        dest = lax.rem(z + i, nz)
        lane = lax.broadcasted_iota(jnp.int32, pos_t.shape, 1)
        each = tok // 128
        there = [
            jnp.concatenate(
                [
                    jnp.sum(
                        jnp.where(lane == (2 * dest + h) * each + e, pos_t, 0.0), 1, keepdims=True
                    )
                    for e in range(each)
                ],
                0,
            )
            for h in range(2)
        ]
        cols = lax.broadcasted_iota(jnp.int32, (tok, piece), 1).astype(F32)

        def inner(t, sums):
            rows = bn[pl.ds(pl.multiple_of(t * piece, piece), piece), :]
            out = []
            for h in range(2):
                hot = jnp.where(there[h] - (t * piece).astype(F32) == cols, 1.0, 0.0).astype(BF16)
                out.append(sums[h] + jnp.dot(hot, rows, preferred_element_type=F32))
            return tuple(out)

        zero = jnp.zeros((tok, bv.shape[0]), F32)
        a, b = lax.fori_loop(0, n_buf // piece, inner, (zero, zero))
        return jnp.concatenate([a, b], 1).astype(BF16)

    def gather_target():
        for i in range(1, nz):
            ordered[i] = ordered_rows(i)
            way = "up" if i == 1 else "down" if i == nz - 1 else i
            swapped.append(send.go(ordered.at[i], target.at[z], way))
            yield
        target[z] = ordered_rows(0)
        yield

    def gather_other():
        crossed.wait_recv()
        yield from gather_cube(send, bits, ICI3, width, other, names)

    side = gather_target()
    cross = gather_other()
    ready = []

    def advance(count):
        for _ in range(count):
            s = step(ring)
            if s is not None:
                ready.extend([s] if s in (0, half) else [s, -s])

    reduce = reduce_cube(send, bits, names, ICI3, width, first_part, first_total, landed[:n_forward])
    for i, _ in enumerate(reduce):
        if i == 0:
            bn[...] = bv[...].T
        step(side)
        advance(FORWARD_STEPS[0][i])
        if i >= 1:
            step(cross)
    hidden = first_total[at(ICI3, bits)].astype(F32)
    resid = fv[mine, :].astype(F32) + hidden
    rscale = lax.rsqrt(jnp.mean(resid * resid, -1, keepdims=True) + EPS)
    full[at(LEAD, bits)] = (resid * rscale * gain[...]).astype(BF16)
    for i, _ in enumerate(gather_cube(send, bits, ICI4, width, full)):
        step(side)
        advance(FORWARD_STEPS[1][i])
    finish(side)
    finish(cross)
    project(1, lambda k: other[at(names, {}, (k.start, k.size))].reshape(tok, k.size))

    started = []

    def add_logits():
        while ready:
            b = lax.rem(z + nz + ready.pop(0), nz)
            cols = (pl.multiple_of(b * 2 * run, 2 * run), 2 * run)
            rows = full[at(LEAD, {}, cols)].reshape(n_tok, 2 * run)
            prod = jnp.dot(rows, head[b], preferred_element_type=F32)
            lg[...] = lg[...] + prod if started else prod
            started.append(b)

    add_logits()
    for c in swapped:
        c.wait_recv()
    for k in range(nz // 2):
        for s in range(2):
            lanes = slice(s * tw, (s + 1) * tw)
            two = [target[2 * k + i].astype(F32)[:, lanes] for i in range(2)]
            pexp[s * tok : (s + 1) * tok, k * 2 * tw : (k + 1) * 2 * tw] = jnp.concatenate(two, 1)
    t = pexp[...]
    top_p = jnp.max(t, -1, keepdims=True)
    t = jnp.exp(t - top_p)
    pexp[...] = t
    sum_p = jnp.sum(t, -1, keepdims=True)
    for s in ring:
        if s is not None:
            ready.extend([s] if s in (0, half) else [s, -s])
            add_logits()
    t = lg[...]
    top_q = jnp.max(t, -1, keepdims=True)
    t = jnp.exp(t - top_q)
    lg[...] = t
    sum_q = jnp.sum(t, -1, keepdims=True)
    lane = lax.broadcasted_iota(jnp.int32, (n_tok, 128), 1)
    columns = jnp.where(
        lane == 0, top_q, jnp.where(lane == 1, top_p, jnp.where(lane == 2, sum_q, sum_p))
    )
    own[...] = columns.T[0:8]
    back[...] = jnp.zeros(back.shape, F32)
    for i in range(n_tok // 128):
        e = i % (tok // 128)
        line = jnp.where(yhi == i // (tok // 128), tk[e : e + 1], tk2[e : e + 1])
        back[8:9, i * 128 : (i + 1) * 128] = line.astype(F32)
    send.drain()
    exchange_stats(send, own, near, held, far, back)
    columns = back[...].T
    all_q, all_p, tot_q, tot_p, token = (columns[:, i : i + 1] for i in (0, 1, 2, 3, 8))
    q = lg[...] * (jnp.exp(top_q - all_q) / tot_q)
    p = pexp[...] * (jnp.exp(top_p - all_p) / tot_p)
    lane = lax.broadcasted_iota(jnp.int32, (n_tok, n_col), 1)
    shift = tw.bit_length() - 1
    column = first_col() + lane + jnp.left_shift(jnp.right_shift(lane, shift), shift)
    onehot = jnp.where(token.astype(jnp.int32) == column, 1.0, 0.0)
    dl[...] = (q - p + HARD * (q - onehot)).astype(BF16)

    split = n_col // 2
    rows_cut = [(pl.ds(i * split, split), slice(None)) for i in range(2)]

    def make_gh(b, q):
        cols = (pl.multiple_of(b * 2 * run, 2 * run), 2 * run)
        rows = full[at(LEAD, {}, cols)].reshape(n_tok, 2 * run)
        ghp[(b,) + rows_cut[q]] = lax.dot_general(
            dl[:, q * split : (q + 1) * split], rows, TN, preferred_element_type=F32
        ).astype(BF16)

    gh_ups, gh_downs = gh_rings[:half], gh_rings[half:]
    ring = ring_scatter(send, z, nz, ghp, gh_ups, gh_downs, rows_cut, make_gh)
    step(ring)
    step(ring)
    block_rows = head.shape[1]
    for c in range(nz):
        cols = (c * block_rows, block_rows)
        block = lax.dot_general(dl[...], head[c], NT, preferred_element_type=F32).astype(BF16)
        for i, f in enumerate(corners(LEAD)):
            part[at(LEAD, f, cols)] = block[i * BLK : (i + 1) * BLK]
    reduce = reduce_cube(send, bits, LEAD, ICI4, width, part, total, landed[n_forward:])
    for i, _ in enumerate(reduce):
        for _ in range(BACKWARD_STEPS[0][i]):
            step(ring)
    dfinal = total[at(REST, bits)].astype(F32)
    scaled = dfinal * gain[...]
    inner = jnp.sum(scaled * resid, -1, keepdims=True)
    dres[at(LEAD, bits)] = (
        rscale * scaled - resid * (rscale * rscale * rscale / width * inner)
    ).astype(BF16)
    def by_half(a, b):
        return jnp.where(yhi == 0, a, b), jnp.where(yhi == 0, b, a)

    def in_order():
        return jnp.concatenate(by_half(pre[0], pre[1]), 0)

    for i, _ in enumerate(gather_cube(send, bits, ICI4, width, dres)):
        if i == 0:
            v = in_order()
            act[...] = (v * jax.nn.sigmoid(v)).astype(BF16)
        for _ in range(BACKWARD_STEPS[1][i]):
            step(ring)
    finish(ring)

    def dresid(start, size):
        return dres[at(LEAD, {}, (start, size))].reshape(n_tok, size)

    lanes_cut = [(slice(None), pl.ds(i * run, run)) for i in range(2)]

    def make_gf(b, q):
        start = pl.multiple_of((2 * b + yhi) * run, run)
        if q:
            left, right = act[...], dresid(start, run)
        else:
            rows = other[at(names, {}, (start, run))].reshape(tok, run)
            left = dpre[...]
            right = jnp.concatenate(by_half(normed[:, pl.ds(start, run)], rows), 0)
        gfp[(b,) + lanes_cut[q]] = lax.dot_general(
            left, right, TN, preferred_element_type=F32
        ).astype(BF16)

    gf_ups = [head.at[i, 0:units] for i in range(half)]
    gf_downs = [head.at[half + i, 0:units] for i in range(half)]
    last = ring_scatter(send, z, nz, gfp, gf_ups, gf_downs, lanes_cut, make_gf)
    step(last)
    for c in range(4):
        k = pl.ds(c * deep, deep)
        prod = lax.dot_general(dresid(c * deep, deep), w2[:, k], NT, preferred_element_type=F32)
        lg[:, 0:units] = prod if c == 0 else lg[:, 0:units] + prod
    v = in_order()
    sig = jax.nn.sigmoid(v)
    dpre[...] = (lg[:, 0:units] * sig * (1.0 + v * (1.0 - sig))).astype(BF16)
    step(last)

    for i in range(2):
        dl[rows_cut[i]] = ring_result(z, ghp, gh_ups, gh_downs, rows_cut, i).astype(BF16)
    crossed = send.go(dl.at[:, there], ghx, ("col", 0, 1))
    for _ in range(3):
        step(last)
    crossed.wait_recv()
    for k in range(nz):
        src = slice(k * tw, (k + 1) * tw)
        for value, side in ((dl[src, here], yhi), (ghx[src, :], 1 - yhi)):
            gh_out[pl.ds(pl.multiple_of(k * 2 * tw + side * tw, tw), tw), :] = value
    finish(last)
    for i in range(2):
        gf_out[lanes_cut[i]] = ring_result(z, gfp, gf_ups, gf_downs, lanes_cut, i).astype(BF16)
    send.drain()


VM = pl.BlockSpec(memory_space=pltpu.VMEM)
ANY = pl.BlockSpec(memory_space=pl.ANY)
SD = jax.ShapeDtypeStruct


def params(cid):
    return pltpu.CompilerParams(
        collective_id=cid, has_side_effects=True, vmem_limit_bytes=62 * 1024 * 1024
    )


def sems(remote, local):
    dma = pltpu.SemaphoreType.DMA
    return [dma((remote,)), dma((remote,)), dma((local,))]


def call_step(first_col, feats, gain_in, w_in, w_out, gain, hw, buf, pos, toks):
    tok, width = feats.shape
    units = w_in.shape[0]
    run, n_col = hw.shape[0], hw.shape[1] // 2
    nz = lax.axis_size("z")
    tw = buf.shape[0]
    n_tok = 2 * tok
    vm = pltpu.VMEM
    scratch = [
        vm((tok, width), BF16),
        vm((run, n_col), BF16),
        vm((128, 128), F32),
        vm((8, 128), jnp.int32),
        vm((8, 128), jnp.int32),
        vm(w_in.shape, BF16),
        vm(w_out.shape, BF16),
        vm(buf.shape, BF16),
        vm(buf.shape[::-1], BF16),
        vm((tok, width), BF16),
        vm(CUBE[1:] + (BLK, width), BF16),
        vm((2, tok, units), F32),
        vm(CUBE + (BLK, width), BF16),
        vm(CUBE[1:] + (BLK, width), BF16),
        vm(CUBE + (BLK, width), BF16),
        vm((nz, 2 * run, n_col), BF16),
        vm((nz, tok, 2 * tw), BF16),
        vm((nz, tok, 2 * tw), BF16),
        vm((n_tok, n_col), F32),
        vm((n_tok, n_col), F32),
        vm((8, n_tok), F32),
        vm((7, 8, n_tok), F32),
        vm((8, n_tok), F32),
        vm((3, 8, n_tok), F32),
        vm((128, n_tok), F32),
        vm((n_tok, n_col), BF16),
        vm(CUBE + (BLK, width), BF16),
        vm((nz, n_col, 2 * run), BF16),
        vm((n_col, run), BF16),
        vm((nz, units, 2 * run), BF16),
        vm((n_tok, units), BF16),
        vm((n_tok, units), BF16),
    ]
    rings = [vm((n_col, 2 * run), BF16) for _ in range(nz)]
    return pl.pallas_call(
        functools.partial(kernel, run, first_col),
        out_shape=(SD((2 * n_col, run), BF16), SD((units, 2 * run), BF16)),
        in_specs=[ANY, VM, ANY, ANY, VM, VM, ANY, VM, VM],
        out_specs=(VM, VM),
        scratch_shapes=scratch
        + sems(256, 4)
        + rings
        + landing(ICI3, width)
        + landing(ICI4, width),
        compiler_params=params(1),
        cost_estimate=pl.CostEstimate(flops=10**10, bytes_accessed=10**8, transcendentals=0),
        name="distill_step",
    )(feats, gain_in[None], w_in, w_out, gain[None], hw, buf, pos, toks)


def write_kernel(gh, gf, gh_out, gi_out, go_out):
    run = gi_out.shape[1]
    gh_out[...] = gh[...].astype(F32).T
    gi_out[...] = gf[:, 0:run].astype(F32)
    go_out[...] = gf[:, run:].astype(F32)


def call_write(gh, gf):
    run = gh.shape[1]
    half = SD((gf.shape[0], run), F32)
    return pl.pallas_call(
        write_kernel,
        out_shape=(SD((run, gh.shape[0]), F32), half, half),
        in_specs=[VM, VM],
        out_specs=(VM, VM, VM),
        compiler_params=pltpu.CompilerParams(vmem_limit_bytes=32 * 1024 * 1024),
        name="write_out",
    )(gh, gf)


def body(
    features, token_ids, positions, target_buffer, norm_gain, final_gain, w_in, w_out, head_weight
):
    cols = head_weight.shape[1]
    tw = target_buffer.shape[1]

    def first_col():
        block = (lax.axis_index("ylo") * 4 + lax.axis_index("x")) * 2 + lax.axis_index("core")
        return block * cols + lax.axis_index("yhi") * tw

    gh, gf = call_step(
        first_col,
        features,
        norm_gain,
        w_in.T,
        w_out,
        final_gain,
        head_weight,
        target_buffer.T,
        positions.reshape(-1, 128),
        token_ids.reshape(-1, 128),
    )
    gh, gi, go = call_write(gh, gf)
    return (gh, gi.T, go)


def solution(mesh):
    names = ("ylo", "x", "core", "z", "yhi")
    fine = Mesh(mesh.devices.reshape(2, 4, 2, -1, 2), names)
    v = ("ylo", "x", "core")
    d = ("z", "yhi")
    return jax.shard_map(
        body,
        mesh=fine,
        in_specs=(
            P(d, None),
            P(d),
            P(),
            P(None, v + d),
            P(),
            P(),
            P(None, v),
            P(v, None),
            P(d, v),
        ),
        out_specs=(P(d, v), P(d, v), P(v, d)),
        check_vma=False,
    )
```

```python
import functools
import jax
import jax.numpy as jnp
from jax import lax
from jax.experimental import pallas as pl
from jax.experimental.pallas import tpu as pltpu
from jax.sharding import Mesh, PartitionSpec as P

EPS = 1e-05
HARD = 0.5
MESH = pl.DeviceIdType.MESH
LEAD = ("YB", "core", "XA", "YA", "XB")
REST = ("YB", "XA", "YA", "XB")
ICI3 = ("XA", "YA", "XB")
ICI4 = ("XA", "YA", "XB", "YB")
CUBE = (2,) * 5
BLK = 16
F32 = jnp.float32
BF16 = jnp.bfloat16


FORWARD_STEPS = ((1, 1, 1, 0, 1), (1, 1, 1, 1))
BACKWARD_STEPS = ((0, 1, 1, 0, 1, 0), (1, 1, 0, 1))


def place():
    x, ylo, yhi, core, z = (lax.axis_index(n) for n in ("x", "ylo", "yhi", "core", "z"))
    nz = lax.axis_size("z")
    y = 2 * yhi + ylo
    odd = lax.rem(x, 2)
    bits = {
        "core": core,
        "XA": lax.rem(lax.div(x + 1, 2), 2),
        "XB": lax.div(x, 2),
        "YA": lax.rem(lax.div(y + 1, 2), 2),
        "YB": yhi,
    }
    to = {
        "core": {"core": 1 - core},
        "XA": {"x": x + 1 - 2 * odd},
        "XB": {"x": lax.rem(x + 3 + 2 * odd, 4)},
        "YA": {"ylo": 1 - ylo},
        "YB": {"ylo": 1 - ylo, "yhi": 1 - yhi},
        "pair": {"yhi": 1 - yhi},
        "up": {"z": lax.rem(z + 1, nz)},
        "down": {"z": lax.rem(z + nz - 1, nz)},
    }
    for i in range(1, nz):
        to[i] = {"z": lax.rem(z + i, nz)}
    for i in range(4):
        for c in range(2):
            to["row", i, c] = {"x": lax.rem(x + i, 4), "core": lax.rem(core + c, 2)}
    for a in range(2):
        for b in range(2):
            to["col", a, b] = {"ylo": lax.rem(ylo + a, 2), "yhi": lax.rem(yhi + b, 2)}
    return bits, to, z, nz


def at(names, fixed, cols=None):
    where = tuple(fixed.get(n, slice(None)) for n in names)
    return where + (slice(None), slice(None) if cols is None else pl.ds(*cols))


def corners(names):
    out = [{}]
    for n in names:
        out = [dict(o, **{n: v}) for o in out for v in (0, 1)]
    return out


class Sender:
    def __init__(self, send_sem, recv_sem, to):
        self.send_sem, self.recv_sem, self.to = send_sem, recv_sem, to
        self.n = 0
        self.open = []

    def go(self, src, dst, dim):
        n = self.n
        c = pltpu.make_async_remote_copy(
            src_ref=src,
            dst_ref=dst,
            send_sem=self.send_sem.at[n],
            recv_sem=self.recv_sem.at[n],
            device_id=self.to[dim],
            device_id_type=MESH,
        )
        c.start()
        self.n += 1
        self.open.append(c)
        return c

    def drain(self):
        for c in self.open:
            c.wait_send()
        self.open = []


class Local:
    def __init__(self, sem):
        self.sem = sem
        self.n = 0

    def go(self, src, dst):
        c = pltpu.make_async_copy(src, dst, self.sem.at[self.n])
        c.start()
        self.n += 1
        return c


def colours(n, width):
    tiles = width // 128
    edges = [128 * (tiles * k // n) for k in range(n + 1)]
    return [(edges[k], edges[k + 1] - edges[k]) for k in range(n)]


def greet(to, dims):
    barrier = pltpu.get_barrier_semaphore()
    for d in dims:
        pl.semaphore_signal(barrier, inc=1, device_id=to[d], device_id_type=MESH)
    return lambda: pl.semaphore_wait(barrier, len(dims))


def meet(to, dims):
    greet(to, dims)()


def step(thread):
    return next(thread, None)


def finish(thread):
    for _ in thread:
        pass


def region(names, order, bits, j, core):
    fixed = {m: bits[m] for m in order[:j]}
    if j < len(order):
        fixed[order[j]] = 1 - bits[order[j]]
    if core:
        fixed["core"] = bits["core"]
    return fixed, [m for m in names if m not in fixed]


def reduce_cube(send, bits, names, dims, width, part, total, landed):
    rest = tuple(n for n in names if n != "core")
    n = len(dims)
    cuts = colours(n, width)
    orders = [[dims[(k + i) % n] for i in range(n)] for k in range(n)]
    first, second = [], []
    for keep, held in ((1, first), (0, second)):
        for k in range(n):
            d = dims[k]
            bit = 1 - bits[d] if keep else bits[d]
            src = part.at[at(names, {"core": 1 - bits["core"], d: bit}, cuts[k])]
            dst = total.at[at(rest, {d: bit}, cuts[k])]
            held.append(send.go(src, dst, "core"))

    def merge(k, bit):
        d = dims[k]
        for f in corners([m for m in rest if m != d]):
            f = dict(f, **{d: bit})
            w = at(rest, f, cuts[k])
            total[w] = total[w] + part[at(names, dict(f, core=bits["core"]), cuts[k])]

    slots = iter(landed)
    coming = {}

    def start(k, i):
        o = orders[k]
        for j in range(i + 1, n + 1):
            fixed = region(rest, o, bits, j, False)[0]
            fixed[o[i]] = 1 - bits[o[i]]
            slot = next(slots)
            src = total.at[at(rest, fixed, cuts[k])]
            coming[k, i, j] = (send.go(src, slot, o[i]), slot)

    yield
    for k in range(n):
        first[k].wait_recv()
        merge(k, 1 - bits[dims[k]])
        start(k, 0)
    yield
    for k in range(n):
        second[k].wait_recv()
        merge(k, bits[dims[k]])
    for j in range(1, n + 1):
        yield
        for k in range(n):
            fixed, free = region(rest, orders[k], bits, j, False)
            got = [coming[k, i, j] for i in range(j)]
            for c, _ in got:
                c.wait_recv()
            for f in corners(free):
                w = at(rest, dict(f, **fixed), cuts[k])
                value = total[w]
                for _, slot in got:
                    value = value + slot[tuple(f[m] for m in free)]
                total[w] = value
            if j < n:
                start(k, j)


def landing(dims, width):
    n = len(dims)
    cuts = colours(n, width)

    def room(k, i):
        return [
            pltpu.VMEM((2,) * (n - 1 - j) + (BLK, cuts[k][1]), BF16) for j in range(i + 1, n + 1)
        ]

    return [slot for i in range(n) for k in range(n) for slot in room(k, i)]


def gather_cube(send, bits, dims, width, full, names=LEAD):
    n = len(dims)
    cuts = colours(n, width)
    orders = [[dims[(k + i) % n] for i in range(n)] for k in range(n)]
    own = full.at[at(names, bits)]
    direct = {d: send.go(own, own, d) for d in dims}
    arriving = [send.go(own, own, "core")]
    coming = {(k, j): [] for k in range(n) for j in range(n)}
    for i in range(n):
        yield
        for k in range(n):
            o = orders[k]
            if i == 0:
                direct[o[0]].wait_recv()
            for c in coming[k, i]:
                c.wait_recv()
            fixed = {m: bits[m] for m in names if m not in o[:i]}
            fixed[o[i]] = 1 - bits[o[i]]
            piece = full.at[at(names, fixed, cuts[k])]
            for j in range(i + 1, n):
                coming[k, j].append(send.go(piece, piece, o[j]))
            arriving.append(send.go(piece, piece, "core"))
    for c in arriving:
        c.wait_recv()


def ring_gather(send, z, nz, full, own, other, late):
    half = nz // 2
    rows = (own, other)

    def block(i, q):
        return full.at[lax.rem(z + nz + i, nz), rows[q]]

    flying = {}

    def hop(s, q):
        for way, sign, short in (("up", -1, 0), ("down", 1, 1)):
            if s and (s < half or q == short):
                flying[way, q].wait_recv()
            if s + 1 < half or (s + 1 == half and q == short):
                flying[way, q] = send.go(block(sign * s, q), block(sign * s, q), way)

    hop(0, 0)
    yield None
    hop(1, 0)
    yield None
    late.wait_recv()
    hop(0, 1)
    yield 0
    for s in range(1, half + 1):
        if s + 1 <= half:
            hop(s + 1, 0)
            yield None
        hop(s, 1)
        yield s


def ring_scatter(send, z, nz, part, ups, downs, cut, prepare):
    half = nz // 2
    made = set()

    def mine(i, q):
        b = lax.rem(z + nz + i, nz)
        if (i % nz, q) not in made:
            made.add((i % nz, q))
            prepare(b, q)
        return part.at[(b,) + cut[q]]

    flying = {}
    ways = (("up", ups, 1), ("down", downs, -1))
    for q in (1, 0):
        for way, landed, sign in ways:
            s = 0 if q == (0 if way == "up" else 1) else 1
            if s < half:
                flying[way, s, q] = send.go(mine(sign * (half - s), q), landed[s].at[cut[q]], way)
        yield
    up = [(1, 1), (0, 0)] + [t for s in range(2, half) for t in ((s, 1), (s - 1, 0))] + [(half - 1, 0)]
    order = [t for t in dict.fromkeys(up) if t[0] < half]
    down = [(0, 1)] + [t for s in range(1, half) for t in ((s, 0), (s, 1))]
    for event in zip(order, down):
        for (way, landed, sign), (s, q) in zip(ways, event):
            own = mine(sign * (half - 1 - s), q)
            flying[way, s, q].wait_recv()
            if s + 1 < half:
                ref = landed[s].at[cut[q]]
                ref[...] = ref[...] + own[...]
                flying[way, s + 1, q] = send.go(ref, landed[s + 1].at[cut[q]], way)
        yield
    for q in range(2):
        mine(0, q)


def ring_result(z, part, ups, downs, cut, q):
    total = part[(z,) + cut[q]].astype(F32)
    sides = (ups, downs) if len(ups) > 1 else ((ups, downs)[q],)
    for side in sides:
        total = total + side[-1][cut[q]].astype(F32)
    return total


def runs_of(value, parity, tw):
    out = []
    for k in range(value.shape[1] // (4 * tw)):
        starts = [(2 * (2 * k + i) + parity) * tw for i in range(2)]
        out.append(jnp.concatenate([value[:, s : s + tw] for s in starts], 1))
    return jnp.concatenate(out, 1)


def own_row(bits):
    r = bits["core"]
    for n in ("XA", "YA", "XB"):
        r = 2 * r + bits[n]
    return r * BLK


def exchange_stats(send, own, near, held, far, out):
    def merge(src, slots, peers, dst):
        flying = [send.go(src, slots.at[i], p) for i, p in enumerate(peers)]
        for c in flying:
            c.wait_recv()
        parts = [src[...]] + [slots[i] for i in range(len(peers))]
        tops = [p[0:2] for p in parts]
        top = functools.reduce(jnp.maximum, tops)
        total = functools.reduce(
            jnp.add, [p[2:4] * jnp.exp(t - top) for p, t in zip(parts, tops)]
        )
        dst[0:2] = top
        dst[2:4] = total

    held[4:8] = jnp.zeros((4, held.shape[1]), F32)
    merge(own, near, [("row", i, c) for i in range(4) for c in range(2) if i or c], held)
    merge(held, far, [("col", a, b) for a in range(2) for b in range(2) if a or b], out)


NT = (((1,), (1,)), ((), ()))
TN = (((0,), (0,)), ((), ()))


def kernel(
    run, first_col,
    feats, gain_in, w_in, w_out, gain, hw, buf, pos, toks,
    gh_out, gf_out,
    fv, hs, pp, tk, tk2, w1, w2, bv, bn, normed, other, pre, part, total, full, head, ordered, target,
    pexp, lg, own, near, held, far, back, dl, dres, ghp, ghx, gfp, act, dpre,
    send_sem, recv_sem, local_sem, *landed,
):
    bits, to, z, nz = place()
    yhi = bits["YB"]
    tok, width = fv.shape
    n_tok = 2 * tok
    n_col = head.shape[2]
    units = w1.shape[0]
    tw = bv.shape[0]
    half = nz // 2
    names = LEAD[1:]
    gh_rings, landed = landed[:nz], landed[nz:]
    n_forward = len(landing(ICI3, width))
    peers = [("row", i, c) for i in range(4) for c in range(2) if i or c]
    peers += [("col", a, b) for a in range(2) for b in range(2) if a or b]
    greeted = greet(to, peers + ["up", "down"] + list(range(2, nz - 1)))
    local = Local(local_sem)
    got_f = local.go(feats, fv)
    got_w1 = local.go(w_in, w1)
    got_w2 = local.go(w_out, w2)
    got_b = local.go(buf, bv)

    here = pl.ds(pl.multiple_of(yhi * run, run), run)
    there = pl.ds(pl.multiple_of((1 - yhi) * run, run), run)
    both = hw[...].astype(F32)
    both = [runs_of(both, p, tw) for p in range(2)]
    head[z, here] = jnp.where(yhi == 0, both[0], both[1]).astype(BF16)
    hs[...] = jnp.where(yhi == 0, both[1], both[0]).astype(BF16)
    tk[...] = jnp.zeros(tk.shape, jnp.int32)
    tk[0 : toks.shape[0]] = toks[...]
    pp[...] = jnp.zeros(pp.shape, F32)
    pp[0 : pos.shape[0]] = pos[...].astype(F32)

    greeted()
    send = Sender(send_sem, recv_sem, to)
    late = send.go(hs, head.at[z, here], "pair")
    ring = ring_gather(send, z, nz, head, here, there, late)
    step(ring)
    swapped = [send.go(tk, tk2, "pair")]
    got_f.wait()
    chunk = 64

    def norm_rows(i, _):
        rows = pl.ds(pl.multiple_of(i * chunk, chunk), chunk)
        x = fv[rows, :].astype(F32)
        r = lax.rsqrt(jnp.mean(x * x, -1, keepdims=True) + EPS)
        normed[rows, :] = (x * r * gain_in[...]).astype(BF16)
        return 0

    lax.fori_loop(0, tok // chunk, norm_rows, 0)
    mine = pl.ds(pl.multiple_of(own_row(bits), BLK), BLK)
    crossed = send.go(normed.at[mine], other.at[at(names, bits)], "YB")

    deep = width // 4

    def project(slot, rows):
        for c in range(4):
            k = pl.ds(c * deep, deep)
            prod = lax.dot_general(rows(k), w1[:, k], NT, preferred_element_type=F32)
            pre[slot] = prod if c == 0 else pre[slot] + prod

    got_w1.wait()
    project(0, lambda k: normed[:, k])
    v = pre[0]
    forward_act = (v * jax.nn.sigmoid(v)).astype(BF16)
    got_w2.wait()
    wide = width // 8
    first_part, first_total = part.at[0], total.at[0]
    for c in range(8):
        cols = (c * wide, wide)
        block = jnp.dot(forward_act, w2[:, pl.ds(*cols)], preferred_element_type=F32).astype(BF16)
        for i, f in enumerate(corners(names)):
            first_part[at(names, f, cols)] = block[i * BLK : (i + 1) * BLK]

    got_b.wait()
    n_buf = bv.shape[1]
    piece = 2048 if n_buf % 2048 == 0 else n_buf
    pos_t = pp[...].T

    def ordered_rows(i):
        dest = lax.rem(z + i, nz)
        lane = lax.broadcasted_iota(jnp.int32, pos_t.shape, 1)
        each = tok // 128
        there = [
            jnp.concatenate(
                [
                    jnp.sum(
                        jnp.where(lane == (2 * dest + h) * each + e, pos_t, 0.0), 1, keepdims=True
                    )
                    for e in range(each)
                ],
                0,
            )
            for h in range(2)
        ]
        cols = lax.broadcasted_iota(jnp.int32, (tok, piece), 1).astype(F32)

        def inner(t, sums):
            rows = bn[pl.ds(pl.multiple_of(t * piece, piece), piece), :]
            out = []
            for h in range(2):
                hot = jnp.where(there[h] - (t * piece).astype(F32) == cols, 1.0, 0.0).astype(BF16)
                out.append(sums[h] + jnp.dot(hot, rows, preferred_element_type=F32))
            return tuple(out)

        zero = jnp.zeros((tok, bv.shape[0]), F32)
        a, b = lax.fori_loop(0, n_buf // piece, inner, (zero, zero))
        return jnp.concatenate([a, b], 1).astype(BF16)

    def gather_target():
        for i in range(1, nz):
            ordered[i] = ordered_rows(i)
            way = "up" if i == 1 else "down" if i == nz - 1 else i
            swapped.append(send.go(ordered.at[i], target.at[z], way))
            yield
        target[z] = ordered_rows(0)
        yield

    def gather_other():
        crossed.wait_recv()
        yield from gather_cube(send, bits, ICI3, width, other, names)

    side = gather_target()
    cross = gather_other()
    ready = []

    def advance(count):
        for _ in range(count):
            s = step(ring)
            if s is not None:
                ready.extend([s] if s in (0, half) else [s, -s])

    reduce = reduce_cube(send, bits, names, ICI3, width, first_part, first_total, landed[:n_forward])
    for i, _ in enumerate(reduce):
        if i == 0:
            bn[...] = bv[...].T
        step(side)
        advance(FORWARD_STEPS[0][i])
        if i >= 1:
            step(cross)
    hidden = first_total[at(ICI3, bits)].astype(F32)
    resid = fv[mine, :].astype(F32) + hidden
    rscale = lax.rsqrt(jnp.mean(resid * resid, -1, keepdims=True) + EPS)
    full[at(LEAD, bits)] = (resid * rscale * gain[...]).astype(BF16)
    for i, _ in enumerate(gather_cube(send, bits, ICI4, width, full)):
        step(side)
        advance(FORWARD_STEPS[1][i])
    finish(side)
    finish(cross)
    project(1, lambda k: other[at(names, {}, (k.start, k.size))].reshape(tok, k.size))

    started = []

    def add_logits():
        while ready:
            b = lax.rem(z + nz + ready.pop(0), nz)
            cols = (pl.multiple_of(b * 2 * run, 2 * run), 2 * run)
            rows = full[at(LEAD, {}, cols)].reshape(n_tok, 2 * run)
            prod = jnp.dot(rows, head[b], preferred_element_type=F32)
            lg[...] = lg[...] + prod if started else prod
            started.append(b)

    add_logits()
    for c in swapped:
        c.wait_recv()
    for k in range(nz // 2):
        for s in range(2):
            lanes = slice(s * tw, (s + 1) * tw)
            two = [target[2 * k + i].astype(F32)[:, lanes] for i in range(2)]
            pexp[s * tok : (s + 1) * tok, k * 2 * tw : (k + 1) * 2 * tw] = jnp.concatenate(two, 1)
    t = pexp[...]
    top_p = jnp.max(t, -1, keepdims=True)
    t = jnp.exp(t - top_p)
    pexp[...] = t
    sum_p = jnp.sum(t, -1, keepdims=True)
    for s in ring:
        if s is not None:
            ready.extend([s] if s in (0, half) else [s, -s])
            add_logits()
    t = lg[...]
    top_q = jnp.max(t, -1, keepdims=True)
    t = jnp.exp(t - top_q)
    lg[...] = t
    sum_q = jnp.sum(t, -1, keepdims=True)
    lane = lax.broadcasted_iota(jnp.int32, (n_tok, 128), 1)
    columns = jnp.where(
        lane == 0, top_q, jnp.where(lane == 1, top_p, jnp.where(lane == 2, sum_q, sum_p))
    )
    own[...] = columns.T[0:8]
    back[...] = jnp.zeros(back.shape, F32)
    for i in range(n_tok // 128):
        e = i % (tok // 128)
        line = jnp.where(yhi == i // (tok // 128), tk[e : e + 1], tk2[e : e + 1])
        back[8:9, i * 128 : (i + 1) * 128] = line.astype(F32)
    send.drain()
    exchange_stats(send, own, near, held, far, back)
    columns = back[...].T
    all_q, all_p, tot_q, tot_p, token = (columns[:, i : i + 1] for i in (0, 1, 2, 3, 8))
    q = lg[...] * (jnp.exp(top_q - all_q) / tot_q)
    p = pexp[...] * (jnp.exp(top_p - all_p) / tot_p)
    lane = lax.broadcasted_iota(jnp.int32, (n_tok, n_col), 1)
    shift = tw.bit_length() - 1
    column = first_col() + lane + jnp.left_shift(jnp.right_shift(lane, shift), shift)
    onehot = jnp.where(token.astype(jnp.int32) == column, 1.0, 0.0)
    dl[...] = (q - p + HARD * (q - onehot)).astype(BF16)

    split = n_col // 2
    rows_cut = [(pl.ds(i * split, split), slice(None)) for i in range(2)]

    def make_gh(b, q):
        cols = (pl.multiple_of(b * 2 * run, 2 * run), 2 * run)
        rows = full[at(LEAD, {}, cols)].reshape(n_tok, 2 * run)
        ghp[(b,) + rows_cut[q]] = lax.dot_general(
            dl[:, q * split : (q + 1) * split], rows, TN, preferred_element_type=F32
        ).astype(BF16)

    gh_ups, gh_downs = gh_rings[:half], gh_rings[half:]
    ring = ring_scatter(send, z, nz, ghp, gh_ups, gh_downs, rows_cut, make_gh)
    step(ring)
    step(ring)
    block_rows = head.shape[1]
    for c in range(nz):
        cols = (c * block_rows, block_rows)
        block = lax.dot_general(dl[...], head[c], NT, preferred_element_type=F32).astype(BF16)
        for i, f in enumerate(corners(LEAD)):
            part[at(LEAD, f, cols)] = block[i * BLK : (i + 1) * BLK]
    reduce = reduce_cube(send, bits, LEAD, ICI4, width, part, total, landed[n_forward:])
    for i, _ in enumerate(reduce):
        for _ in range(BACKWARD_STEPS[0][i]):
            step(ring)
    dfinal = total[at(REST, bits)].astype(F32)
    scaled = dfinal * gain[...]
    inner = jnp.sum(scaled * resid, -1, keepdims=True)
    dres[at(LEAD, bits)] = (
        rscale * scaled - resid * (rscale * rscale * rscale / width * inner)
    ).astype(BF16)
    def by_half(a, b):
        return jnp.where(yhi == 0, a, b), jnp.where(yhi == 0, b, a)

    def in_order():
        return jnp.concatenate(by_half(pre[0], pre[1]), 0)

    for i, _ in enumerate(gather_cube(send, bits, ICI4, width, dres)):
        if i == 0:
            v = in_order()
            act[...] = (v * jax.nn.sigmoid(v)).astype(BF16)
        for _ in range(BACKWARD_STEPS[1][i]):
            step(ring)
    finish(ring)

    def dresid(start, size):
        return dres[at(LEAD, {}, (start, size))].reshape(n_tok, size)

    lanes_cut = [(slice(None), pl.ds(i * run, run)) for i in range(2)]

    def make_gf(b, q):
        start = pl.multiple_of((2 * b + yhi) * run, run)
        if q:
            left, right = act[...], dresid(start, run)
        else:
            rows = other[at(names, {}, (start, run))].reshape(tok, run)
            left = dpre[...]
            right = jnp.concatenate(by_half(normed[:, pl.ds(start, run)], rows), 0)
        gfp[(b,) + lanes_cut[q]] = lax.dot_general(
            left, right, TN, preferred_element_type=F32
        ).astype(BF16)

    gf_ups = [head.at[i, 0:units] for i in range(half)]
    gf_downs = [head.at[half + i, 0:units] for i in range(half)]
    last = ring_scatter(send, z, nz, gfp, gf_ups, gf_downs, lanes_cut, make_gf)
    step(last)
    for c in range(4):
        k = pl.ds(c * deep, deep)
        prod = lax.dot_general(dresid(c * deep, deep), w2[:, k], NT, preferred_element_type=F32)
        lg[:, 0:units] = prod if c == 0 else lg[:, 0:units] + prod
    v = in_order()
    sig = jax.nn.sigmoid(v)
    dpre[...] = (lg[:, 0:units] * sig * (1.0 + v * (1.0 - sig))).astype(BF16)
    step(last)

    for i in range(2):
        dl[rows_cut[i]] = ring_result(z, ghp, gh_ups, gh_downs, rows_cut, i).astype(BF16)
    crossed = send.go(dl.at[:, there], ghx, ("col", 0, 1))
    for _ in range(3):
        step(last)
    crossed.wait_recv()
    for k in range(nz):
        src = slice(k * tw, (k + 1) * tw)
        for value, side in ((dl[src, here], yhi), (ghx[src, :], 1 - yhi)):
            gh_out[pl.ds(pl.multiple_of(k * 2 * tw + side * tw, tw), tw), :] = value
    finish(last)
    for i in range(2):
        gf_out[lanes_cut[i]] = ring_result(z, gfp, gf_ups, gf_downs, lanes_cut, i).astype(BF16)
    send.drain()


VM = pl.BlockSpec(memory_space=pltpu.VMEM)
ANY = pl.BlockSpec(memory_space=pl.ANY)
SD = jax.ShapeDtypeStruct


def params(cid):
    return pltpu.CompilerParams(
        collective_id=cid, has_side_effects=True, vmem_limit_bytes=62 * 1024 * 1024
    )


def sems(remote, local):
    dma = pltpu.SemaphoreType.DMA
    return [dma((remote,)), dma((remote,)), dma((local,))]


def call_step(first_col, feats, gain_in, w_in, w_out, gain, hw, buf, pos, toks):
    tok, width = feats.shape
    units = w_in.shape[0]
    run, n_col = hw.shape[0], hw.shape[1] // 2
    nz = lax.axis_size("z")
    tw = buf.shape[0]
    n_tok = 2 * tok
    vm = pltpu.VMEM
    scratch = [
        vm((tok, width), BF16),
        vm((run, n_col), BF16),
        vm((128, 128), F32),
        vm((8, 128), jnp.int32),
        vm((8, 128), jnp.int32),
        vm(w_in.shape, BF16),
        vm(w_out.shape, BF16),
        vm(buf.shape, BF16),
        vm(buf.shape[::-1], BF16),
        vm((tok, width), BF16),
        vm(CUBE[1:] + (BLK, width), BF16),
        vm((2, tok, units), F32),
        vm(CUBE + (BLK, width), BF16),
        vm(CUBE[1:] + (BLK, width), BF16),
        vm(CUBE + (BLK, width), BF16),
        vm((nz, 2 * run, n_col), BF16),
        vm((nz, tok, 2 * tw), BF16),
        vm((nz, tok, 2 * tw), BF16),
        vm((n_tok, n_col), F32),
        vm((n_tok, n_col), F32),
        vm((8, n_tok), F32),
        vm((7, 8, n_tok), F32),
        vm((8, n_tok), F32),
        vm((3, 8, n_tok), F32),
        vm((128, n_tok), F32),
        vm((n_tok, n_col), BF16),
        vm(CUBE + (BLK, width), BF16),
        vm((nz, n_col, 2 * run), BF16),
        vm((n_col, run), BF16),
        vm((nz, units, 2 * run), BF16),
        vm((n_tok, units), BF16),
        vm((n_tok, units), BF16),
    ]
    rings = [vm((n_col, 2 * run), BF16) for _ in range(nz)]
    return pl.pallas_call(
        functools.partial(kernel, run, first_col),
        out_shape=(SD((2 * n_col, run), BF16), SD((units, 2 * run), BF16)),
        in_specs=[ANY, VM, ANY, ANY, VM, VM, ANY, VM, VM],
        out_specs=(VM, VM),
        scratch_shapes=scratch
        + sems(256, 4)
        + rings
        + landing(ICI3, width)
        + landing(ICI4, width),
        compiler_params=params(1),
        cost_estimate=pl.CostEstimate(flops=10**10, bytes_accessed=10**8, transcendentals=0),
        name="distill_step",
    )(feats, gain_in[None], w_in, w_out, gain[None], hw, buf, pos, toks)


def write_kernel(gh, gf, gh_out, gi_out, go_out):
    run = gi_out.shape[1]
    gh_out[...] = gh[...].astype(F32).T
    gi_out[...] = gf[:, 0:run].astype(F32)
    go_out[...] = gf[:, run:].astype(F32)


def call_write(gh, gf):
    run = gh.shape[1]
    half = SD((gf.shape[0], run), F32)
    return pl.pallas_call(
        write_kernel,
        out_shape=(SD((run, gh.shape[0]), F32), half, half),
        in_specs=[VM, VM],
        out_specs=(VM, VM, VM),
        compiler_params=pltpu.CompilerParams(vmem_limit_bytes=32 * 1024 * 1024),
        name="write_out",
    )(gh, gf)


def body(
    features, token_ids, positions, target_buffer, norm_gain, final_gain, w_in, w_out, head_weight
):
    cols = head_weight.shape[1]
    tw = target_buffer.shape[1]

    def first_col():
        block = (lax.axis_index("ylo") * 4 + lax.axis_index("x")) * 2 + lax.axis_index("core")
        return block * cols + lax.axis_index("yhi") * tw

    gh, gf = call_step(
        first_col,
        features,
        norm_gain,
        w_in.T,
        w_out,
        final_gain,
        head_weight,
        target_buffer.T,
        positions.reshape(-1, 128),
        token_ids.reshape(-1, 128),
    )
    gh, gi, go = call_write(gh, gf)
    return (gh, gi.T, go)


def solution(mesh):
    names = ("ylo", "x", "core", "z", "yhi")
    fine = Mesh(mesh.devices.reshape(2, 4, 2, -1, 2), names)
    v = ("ylo", "x", "core")
    d = ("z", "yhi")
    return jax.shard_map(
        body,
        mesh=fine,
        in_specs=(
            P(d, None),
            P(d),
            P(),
            P(None, v + d),
            P(),
            P(),
            P(None, v),
            P(v, None),
            P(d, v),
        ),
        out_specs=(P(d, v), P(d, v), P(v, d)),
        check_vma=False,
    )
```
